1024 devices in a mesh: ty: 32 (over x, z_hi, y), tx: 16 (over z_lo), corner: 2 (over core).
Axes of the slice: x: 4, y: 4, z: 32 (z_hi: 2, z_lo: 16; z = z_hi * 16 + z_lo), core: 2. Of those that a mesh axis runs over, the one named last changes fastest.
Arguments:
- level_init: int32 [8192, 4096], P('ty', 'tx'), may hold values from -64 to 64
- target: int32 [8192, 4096], P('ty', 'tx'), may hold values 0 or 1
- kernels: float32 [2, 5, 2, 128, 128], P('corner'), may hold values from -12 to 12
- corner_doses: float32 [2], P('corner'), may hold values from 0.7 to 1.4
Outputs:
- resist: float32 [2, 8192, 4096], P('corner', 'ty', 'tx')
- level_set: float32 [8192, 4096], P('ty', 'tx')
The draws below stay inside these ranges and needn't reach their ends.
All inputs are finite; a program needn't handle non-finite values. No bound on the sum of `target` on one device may be relied on, other than what follows from the above.
Results may differ from the reference program's by a relative error of at most 0.015.
The reference program's roundings to bfloat16 on the way count: a program that leaves them out, or rounds other values in their place, can miss the bound.
Values may be sent and summed in bfloat16 or wider, within the bound.
A program may use at most 32 MiB of HBM per device.

```python
import math
import jax
import jax.numpy as jnp
from jax import lax

TILE = 256
HALO = 128
KF = 128
KERNELS = 5
LS_STEPS = 3
WIN = 512
NY = 8192
NX = 4096
CORNERS = 2
N_TY = 32
N_TX = 16


def place_ends(values, rng, smallest, high):
    shape = values.shape
    spot = [jax.random.randint(jax.random.fold_in(rng, axis), (), 0, shape[axis]) for axis in range(len(shape))]
    values = values.at[tuple(spot)].set(smallest)
    longest = shape.index(max(shape))
    spot[longest] = (spot[longest] + 1) % shape[longest]
    return values.at[tuple(spot)].set(high)


def level_of(stream_key, dims, shards, low, top_value):
    level = 1.0
    for axis_at, shards_of in shards:
        steps = jax.random.uniform(jax.random.fold_in(jax.random.fold_in(stream_key, 6), axis_at), (shards_of,), jnp.float32, low / len(shards), top_value / len(shards))
        level = level * jnp.repeat(jnp.exp(steps), dims[axis_at] // shards_of).reshape((-1,) + (1,) * (len(dims) - 1 - axis_at))
    return level


def gaussian(rng, shape, scale, most, pieces=(), held_as=jnp.bfloat16):
    entries = scale * jax.random.normal(rng, shape, jnp.float32)
    if pieces:
        entries = entries * level_of(rng, shape, pieces, -0.22, 0.18)
    return jnp.clip(entries, -most, most).astype(held_as)


def setup_inputs(seed: int = 0) -> dict:
    streams_of = jax.random.split(jax.random.key(seed), 5)
    level_init = place_ends(jax.random.randint(streams_of[0], (NY, NX), -64, 65), jax.random.fold_in(streams_of[0], 1), -64, 64).astype(jnp.int32)
    target = place_ends((jax.random.randint(streams_of[1], (NY, NX), 0, 2) < 1).astype(jnp.int32), jax.random.fold_in(streams_of[1], 1), 0, 1)
    kernels = gaussian(streams_of[2], (CORNERS, KERNELS, 2, KF, KF), 2.0, 12.0, ((0, 2),), jnp.float32)
    corner_doses = jnp.clip(jnp.exp(math.log(1.4) - 0.6931472 * jax.random.uniform(streams_of[3], (CORNERS,), jnp.float32) ** level_of(streams_of[3], (CORNERS,), ((0, 2),), -0.2, 0.2)), 0.7, 1.4)
    return dict(level_init=level_init, target=target, kernels=kernels, corner_doses=corner_doses)


STEEPNESS = 4.0
THRESHOLD = 1.0
SPEED_GAIN = 4.0
SMOOTHING = 0.24
GRAD_FLOOR = 0.25

def make_tables(window, freqs, margin, tile):
    shifts = jnp.arange(freqs, dtype=jnp.int32) - freqs // 2
    places = jnp.arange(window, dtype=jnp.int32)
    phases = shifts[:, None] * places[None, :] % window
    angles = 2.0 * math.pi / window * phases.astype(jnp.float32)
    scaled = 1.0 / math.sqrt(window)
    fwd_cos = (jnp.cos(angles) * scaled).astype(jnp.bfloat16)
    fwd_sin = (-jnp.sin(angles) * scaled).astype(jnp.bfloat16)
    inner = angles[:, margin:margin + tile].T
    inv_cos = (jnp.cos(inner) * scaled).astype(jnp.bfloat16)
    inv_sin = (jnp.sin(inner) * scaled).astype(jnp.bfloat16)
    return (fwd_cos, fwd_sin, inv_cos, inv_sin)

def matmul(left, right):
    return jnp.dot(left, right, preferred_element_type=jnp.float32)

def batched(form, left, right):
    return jnp.einsum(form, left.astype(jnp.float32), right.astype(jnp.float32), precision=lax.Precision.HIGHEST)

def tile_pass(win_data, goal, kernel_re, kernel_im, doses_col, tables):
    fwd_cos, fwd_sin, inv_cos, inv_sin = tables
    freqs = fwd_cos.shape[0]
    lift = matmul(jnp.concatenate([fwd_cos, fwd_sin], axis=0), win_data).astype(jnp.bfloat16)
    lift_re = lift[:freqs]
    lift_im = lift[freqs:]
    spec_re = matmul(lift_re, fwd_cos.T) - matmul(lift_im, fwd_sin.T)
    spec_im = matmul(lift_re, fwd_sin.T) + matmul(lift_im, fwd_cos.T)
    blur_re = (kernel_re * spec_re - kernel_im * spec_im).astype(jnp.bfloat16)
    blur_im = (kernel_re * spec_im + kernel_im * spec_re).astype(jnp.bfloat16)
    proj_re = (batched('rj,gjk->grk', inv_cos, blur_re) - batched('rj,gjk->grk', inv_sin, blur_im)).astype(jnp.bfloat16)
    proj_im = (batched('rj,gjk->grk', inv_cos, blur_im) + batched('rj,gjk->grk', inv_sin, blur_re)).astype(jnp.bfloat16)
    field_re = batched('grj,cj->grc', proj_re, inv_cos) - batched('grj,cj->grc', proj_im, inv_sin)
    field_im = batched('grj,cj->grc', proj_re, inv_sin) + batched('grj,cj->grc', proj_im, inv_cos)
    groups = doses_col.shape[0]
    tile = field_re.shape[1]
    grouped = (groups, -1, tile, tile)
    power = (field_re * field_re + field_im * field_im).reshape(grouped)
    intensity = lax.optimization_barrier(jnp.sum(power, axis=1))
    dose_col = doses_col[:, None, None]
    resist = jax.nn.sigmoid(STEEPNESS * (dose_col * intensity - THRESHOLD))
    sens = 2.0 * (resist - goal) * STEEPNESS * dose_col * resist * (1.0 - resist)
    adj_re = (2.0 * sens[:, None] * field_re.reshape(grouped)).reshape(field_re.shape).astype(jnp.bfloat16)
    adj_im = (2.0 * sens[:, None] * field_im.reshape(grouped)).reshape(field_im.shape).astype(jnp.bfloat16)
    back_re = (batched('grc,cj->grj', adj_re, inv_cos) + batched('grc,cj->grj', adj_im, inv_sin)).astype(jnp.bfloat16)
    back_im = (batched('grc,cj->grj', adj_im, inv_cos) - batched('grc,cj->grj', adj_re, inv_sin)).astype(jnp.bfloat16)
    grad_blur_re = batched('rj,grk->gjk', inv_cos, back_re) + batched('rj,grk->gjk', inv_sin, back_im)
    grad_blur_im = batched('rj,grk->gjk', inv_cos, back_im) - batched('rj,grk->gjk', inv_sin, back_re)
    grad_spec_re = lax.optimization_barrier(jnp.sum(kernel_re * grad_blur_re + kernel_im * grad_blur_im, axis=0))
    grad_spec_im = lax.optimization_barrier(jnp.sum(kernel_re * grad_blur_im - kernel_im * grad_blur_re, axis=0))
    return (resist, grad_spec_re, grad_spec_im)

def window_grad(grad_spec_re, grad_spec_im, tables):
    fwd_cos, fwd_sin = (tables[0], tables[1])
    spec_low_re = grad_spec_re.astype(jnp.bfloat16)
    spec_low_im = grad_spec_im.astype(jnp.bfloat16)
    grad_lift_re = (matmul(spec_low_re, fwd_cos) + matmul(spec_low_im, fwd_sin)).astype(jnp.bfloat16)
    grad_lift_im = (matmul(spec_low_im, fwd_cos) - matmul(spec_low_re, fwd_sin)).astype(jnp.bfloat16)
    stacked = jnp.concatenate([fwd_cos, fwd_sin], axis=0)
    grad_lift = jnp.concatenate([grad_lift_re, grad_lift_im], axis=0)
    result = lax.dot_general(stacked, grad_lift, (((0,), (0,)), ((), ())), preferred_element_type=jnp.float32)
    return result.astype(jnp.bfloat16)

def advance(padded, speed):
    centre = padded[1:-1, 1:-1]
    above_cells = padded[:-2, 1:-1]
    below_cells = padded[2:, 1:-1]
    left_cells = padded[1:-1, :-2]
    right_cells = padded[1:-1, 2:]
    slope_y = 0.5 * (below_cells - above_cells)
    slope_x = 0.5 * (right_cells - left_cells)
    spread = above_cells + below_cells + left_cells + right_cells - 4.0 * centre
    return centre - SPEED_GAIN * speed * jnp.sqrt(GRAD_FLOOR + slope_y * slope_y + slope_x * slope_x) + SMOOTHING * spread

def reference(level_init, target, kernels, corner_doses):
    tile = TILE
    margin = HALO
    window = WIN
    freqs = KF
    tables = make_tables(window, freqs, margin, tile)
    level = level_init.astype(jnp.float32) * 0.125
    trans = jnp.tanh(0.25 * level)
    padded = jnp.pad(trans.astype(jnp.bfloat16), margin)
    kernel_re = kernels[:, :, 0].reshape(-1, freqs, freqs)
    kernel_im = kernels[:, :, 1].reshape(-1, freqs, freqs)
    goals = target.astype(jnp.float32)

    def per_tile(index):
        row_start = (index // N_TX * tile).astype(jnp.int32)
        col_start = (index % N_TX * tile).astype(jnp.int32)
        win_data = lax.dynamic_slice(padded, (row_start, col_start), (window, window))
        goal = lax.dynamic_slice(goals, (row_start, col_start), (tile, tile))
        resist_tile, grad_spec_re, grad_spec_im = tile_pass(win_data, goal, kernel_re, kernel_im, corner_doses, tables)
        return (resist_tile, window_grad(grad_spec_re, grad_spec_im, tables))
    count = N_TY * N_TX
    resist_all, windows = lax.map(per_tile, jnp.arange(count, dtype=jnp.int32))
    total = jnp.zeros((NY + 2 * margin, NX + 2 * margin), jnp.float32)

    def add_window(index, total):
        row_start = (index // N_TX * tile).astype(jnp.int32)
        col_start = (index % N_TX * tile).astype(jnp.int32)
        piece = windows[index].astype(jnp.float32)
        current = lax.dynamic_slice(total, (row_start, col_start), (window, window))
        return lax.dynamic_update_slice(total, current + piece, (row_start, col_start))
    total = lax.fori_loop(0, count, add_window, total)
    grad_trans = total[margin:margin + NY, margin:margin + NX]
    speed = grad_trans * 0.25 * (1.0 - trans * trans)
    for repeat in range(LS_STEPS):
        level = advance(jnp.pad(level, 1), speed)
    resist = resist_all.reshape(N_TY, N_TX, CORNERS, tile, tile).transpose(2, 0, 3, 1, 4).reshape(CORNERS, NY, NX)
    return (resist, level)
```

```python
import math

import jax
import jax.numpy as jnp
import ml_dtypes
import numpy as np
from jax import lax
from jax.experimental import pallas as pl
from jax.experimental.pallas import tpu as pltpu
from jax.sharding import PartitionSpec as P

TILE = 256
HALO = 128
KF = 128
WIN = 512
KERNELS = 5
LS_STEPS = 3

STEEPNESS = 4.0
THRESHOLD = 1.0
SPEED_GAIN = 4.0
SMOOTHING = 0.24
GRAD_FLOOR = 0.25

MESH = pl.DeviceIdType.MESH
F32 = jnp.float32
BF16 = jnp.bfloat16

EXT = 144
LANES = 384


def wide_tables():
    shifts = np.arange(KF, dtype=np.int32) - KF // 2
    places = np.arange(WIN, dtype=np.int32)
    phases = (shifts[:, None] * places[None, :]) % WIN
    angles = np.float32(2.0 * math.pi / WIN) * phases.astype(np.float32)
    scaled = np.float32(1.0 / math.sqrt(WIN))
    fc = np.cos(angles, dtype=np.float32) * scaled
    fs = -np.sin(angles, dtype=np.float32) * scaled
    inner = angles[:, HALO : HALO + TILE].T
    ic = np.cos(inner, dtype=np.float32) * scaled
    isn = np.sin(inner, dtype=np.float32) * scaled
    fwd = np.concatenate([fc, fs], 0)
    turn = np.concatenate([-fs, fc], 0)
    to_field = np.concatenate(
        [np.concatenate([ic.T, isn.T], 1), np.concatenate([-isn.T, ic.T], 1)], 0
    )
    inv = np.concatenate([ic, isn], 1)
    ft = fwd.T
    lo, hi = HALO, HALO + 128
    own = [
        np.concatenate([ft[lo:hi], ft[hi : hi + 8], ft[lo - 8 : lo]], 0),
        np.concatenate([ft[hi : hi + 128], ft[hi + 128 : hi + 136], ft[hi - 8 : hi]], 0),
    ]
    strip = [ft[368:512], np.concatenate([ft[128:144], ft[0:128]], 0)]
    cross = [
        np.concatenate([fwd[:, 384:512], fwd[:, 256:384]], 1),
        fwd[:, 0:256],
    ]
    a = np.concatenate([fwd, turn, to_field], 0)
    b = np.concatenate([ft, inv, to_field.T, inv.T] + own + strip + cross, 0)
    return a.astype(ml_dtypes.bfloat16), b.astype(ml_dtypes.bfloat16)


A_FWD, A_TURN, A_FIELD, A_ROWS = 0, 256, 512, 768
B_FT, B_INV, B_BACK, B_INVT, B_OWN = 0, 512, 768, 1280, 1536
B_STRIP = B_OWN + 2 * EXT
B_CROSS = B_STRIP + 2 * EXT
B_ROWS = B_CROSS + 512


def mm(x, y):
    return jnp.dot(x, y, preferred_element_type=F32)


def mm_nt(x, y):
    return lax.dot_general(x, y, (((1,), (1,)), ((), ())), preferred_element_type=F32)


def one_hot(shape, pairs):
    rows = lax.broadcasted_iota(jnp.int32, shape, 0)
    cols = lax.broadcasted_iota(jnp.int32, shape, 1)
    hit = jnp.zeros(shape, F32)
    for r, c in pairs:
        hit = jnp.where((rows == r) & (cols == c), 1.0, hit)
    return hit.astype(BF16)


def kernel(
    n_ty,
    n_tx,
    level_hbm,
    target_hbm,
    kern_hbm,
    dose_ref,
    a_hbm,
    b_hbm,
    resist_hbm,
    out_hbm,
    level_i,
    target_i,
    kern,
    ta,
    tb,
    win,
    trw,
    spec,
    fields,
    inten,
    sens2,
    resist,
    gacc,
    gother,
    hbuf,
    lift,
    glift,
    msg_s,
    msg_r,
    small_s,
    small_r,
    final,
    in_sem,
    out_sem,
    send,
    s_side,
    s_far,
    s_fan,
    s_part,
    s_corner,
    s_spec,
    s_msg,
    s_small,
    s_final,
):
    a, b, c = lax.axis_index("ty"), lax.axis_index("tx"), lax.axis_index("corner")
    has_l, has_r = b > 0, b < n_tx - 1
    up_ok, dn_ok = a > 0, a < n_ty - 1
    is0 = c == 0
    send_ok = jnp.where(is0, dn_ok.astype(jnp.int32), up_ok.astype(jnp.int32)) > 0
    recv_ok = jnp.where(is0, up_ok.astype(jnp.int32), dn_ok.astype(jnp.int32)) > 0
    ar = a + 1 - 2 * c
    bl, br = jnp.maximum(b - 1, 0), jnp.minimum(b + 1, n_tx - 1)
    zl, zr = jnp.where(has_l, 0, 1), jnp.where(has_r, 0, 1)
    other = 1 - c
    left, right, partner = (a, b - 1, c), (a, b + 1, c), (a, b, other)

    def local(src, dst, sem):
        cp = pltpu.make_async_copy(src, dst, sem)
        cp.start()
        return cp

    def remote(i, src, dst, rsem, dev):
        return pltpu.make_async_remote_copy(
            src_ref=src,
            dst_ref=dst,
            send_sem=send.at[i],
            recv_sem=rsem,
            device_id=dev,
            device_id_type=MESH,
        )

    def arrived(dst, rsem):
        pltpu.make_async_remote_copy(
            src_ref=dst,
            dst_ref=dst,
            send_sem=send.at[0],
            recv_sem=rsem,
            device_id=partner,
            device_id_type=MESH,
        ).wait_recv()

    cp_level = local(level_hbm, level_i, in_sem.at[0])
    cp_a = local(a_hbm, ta, in_sem.at[1])
    cp_kern = local(kern_hbm, kern, in_sem.at[2])
    cp_b = local(b_hbm, tb, in_sem.at[3])
    cp_target = local(target_hbm, target_i, in_sem.at[4])

    barrier = pltpu.get_barrier_semaphore()

    def hello(dev):
        pl.semaphore_signal(barrier, inc=1, device_id=dev, device_id_type=MESH)

    @pl.when(up_ok)
    def _():
        hello((a - 1, bl, 0))
        hello((a - 1, br, 0))

    @pl.when(dn_ok)
    def _():
        hello((a + 1, bl, 1))
        hello((a + 1, br, 1))

    hello(partner)

    @pl.when(has_l)
    def _():
        hello((a, b - 1, 0))
        hello((a, b - 1, 1))

    @pl.when(has_r)
    def _():
        hello((a, b + 1, 0))
        hello((a, b + 1, 1))

    cp_level.wait()
    level0 = level_i[...].astype(F32) * 0.125
    low = level0.astype(BF16)
    win[1, 128:384] = low[:, :128]
    win[2, 128:384] = low[:, 128:]

    wanted = (
        1
        + 2 * has_l.astype(jnp.int32)
        + 2 * has_r.astype(jnp.int32)
        + 4 * send_ok.astype(jnp.int32)
    )
    pl.semaphore_wait(barrier, wanted)

    srow = pl.multiple_of(256 - 128 * c, 128)
    hrow = pl.multiple_of(384 * c, 128)
    fl = remote(0, win.at[1, pl.ds(srow, 128)], win.at[jnp.where(has_l, 3, 1), pl.ds(hrow, 128)], s_far.at[1 - zl], (ar, bl, c))
    fr = remote(1, win.at[2, pl.ds(srow, 128)], win.at[jnp.where(has_r, 0, 2), pl.ds(hrow, 128)], s_far.at[zr], (ar, br, c))
    sl = remote(2, win.at[1, pl.ds(128, 256)], win.at[3, pl.ds(128, 256)], s_side.at[1], left)
    sr = remote(3, win.at[2, pl.ds(128, 256)], win.at[0, pl.ds(128, 256)], s_side.at[0], right)

    @pl.when(send_ok)
    def _():
        fl.start()
        fr.start()

    @pl.when(has_l)
    def _():
        sl.start()

    @pl.when(has_r)
    def _():
        sr.start()

    @pl.when(jnp.logical_not(has_l))
    def _():
        win[0] = jnp.zeros((WIN, 128), BF16)
        hbuf[0] = jnp.zeros((KF, 256), BF16)

    @pl.when(jnp.logical_not(has_r))
    def _():
        win[3] = jnp.zeros((WIN, 128), BF16)
        hbuf[2] = jnp.zeros((KF, 256), BF16)

    for q, ok in ((0, up_ok), (384, dn_ok)):
        @pl.when(jnp.logical_not(ok))
        def _(q=q):
            for blk in range(4):
                win[blk, q : q + 128] = jnp.zeros((128, 128), BF16)

    @pl.when(jnp.logical_not(recv_ok))
    def _():
        msg_r[...] = jnp.zeros_like(msg_r)

    small_ok = jnp.where(is0, dn_ok.astype(jnp.int32), up_ok.astype(jnp.int32)) > 0

    @pl.when(jnp.logical_not(small_ok))
    def _():
        small_r[...] = jnp.zeros_like(small_r)

    def to_trans(blk, r0, rows):
        x = win[blk, r0 : r0 + rows].astype(F32)
        trw[r0 : r0 + rows, blk * 128 : blk * 128 + 128] = jnp.tanh(0.25 * x).astype(BF16)

    to_trans(1, 128, 256)
    to_trans(2, 128, 256)

    @pl.when(has_l)
    def _():
        arrived(win.at[0, pl.ds(128, 256)], s_side.at[0])

    to_trans(0, 128, 256)

    @pl.when(has_r)
    def _():
        arrived(win.at[3, pl.ds(128, 256)], s_side.at[1])

    to_trans(3, 128, 256)
    cp_a.wait()
    cp_b.wait()
    cp_kern.wait()
    cp_target.wait()
    lift[...] = mm(ta[A_FWD : A_FWD + 256, 128:384], trw[128:384, :])

    blk_l, blk_r = jnp.where(has_l, 0, 1), jnp.where(has_r, 3, 2)
    got_l, got_r = win.at[blk_l, pl.ds(hrow, 128)], win.at[blk_r, pl.ds(hrow, 128)]
    pl_ = remote(4, got_l, got_l, s_part.at[0], partner)
    pr_ = remote(5, got_r, got_r, s_part.at[1], partner)
    fan_l = [remote(6 + d, got_l, win.at[2, pl.ds(hrow, 128)], s_fan.at[c, 1], (a, b - 1, d)) for d in (0, 1)]
    fan_r = [remote(8 + d, got_r, win.at[1, pl.ds(hrow, 128)], s_fan.at[c, 0], (a, b + 1, d)) for d in (0, 1)]

    @pl.when(recv_ok)
    def _():
        arrived(got_l, s_far.at[0])

        @pl.when(has_l)
        def _():
            fan_l[0].start()
            fan_l[1].start()

        pl_.start()
        arrived(got_r, s_far.at[1])

        @pl.when(has_r)
        def _():
            fan_r[0].start()
            fan_r[1].start()

        pr_.start()

    @pl.when(small_ok)
    def _():
        orow = pl.multiple_of(384 * other, 128)
        arrived(win.at[blk_l, pl.ds(orow, 128)], s_part.at[0])
        arrived(win.at[blk_r, pl.ds(orow, 128)], s_part.at[1])

    for d, ok in ((0, up_ok), (1, dn_ok)):
        @pl.when(ok & has_l)
        def _(d=d):
            arrived(win.at[1, pl.ds(384 * d, 128)], s_fan.at[d, 0])

        @pl.when(ok & has_r)
        def _(d=d):
            arrived(win.at[2, pl.ds(384 * d, 128)], s_fan.at[d, 1])

    for blk in range(4):
        to_trans(blk, 0, 128)
        to_trans(blk, 384, 128)
    lift_b = (
        lift[...]
        + mm(ta[A_FWD : A_FWD + 256, 0:128], trw[0:128, :])
        + mm(ta[A_FWD : A_FWD + 256, 384:512], trw[384:512, :])
    ).astype(BF16)
    s = mm(lift_b, tb[B_FT : B_FT + 512])
    spec[0] = s[:128, :128] - s[128:, 128:]
    spec[1] = s[:128, 128:] + s[128:, :128]

    dose = dose_ref[0]
    inten[...] = jnp.zeros_like(inten)

    def ahead(k, _):
        kr, ki = kern[0, k, 0], kern[0, k, 1]
        sre, sim = spec[0], spec[1]
        bre = (kr * sre - ki * sim).astype(BF16)
        bim = (kr * sim + ki * sre).astype(BF16)
        blur = jnp.concatenate(
            [jnp.concatenate([bre, bim], 1), jnp.concatenate([-bim, bre], 1)], 0
        )
        proj = mm(tb[B_INV : B_INV + 256], blur).astype(BF16)
        field = mm(proj, ta[A_FIELD : A_FIELD + 256])
        fields[k] = field
        fre, fim = field[:, :256], field[:, 256:]
        inten[...] += fre * fre + fim * fim
        return 0

    lax.fori_loop(0, KERNELS, ahead, 0)

    res = jax.nn.sigmoid(STEEPNESS * (dose * inten[...] - THRESHOLD))
    resist[...] = res
    cp_resist = local(resist, resist_hbm.at[0], out_sem.at[0])
    goal = target_i[...].astype(F32)
    sens2[...] = 2.0 * (2.0 * (res - goal) * STEEPNESS * dose * res * (1.0 - res))
    gacc[...] = jnp.zeros_like(gacc)

    def back(k, _):
        kr, ki = kern[0, k, 0], kern[0, k, 1]
        s2 = sens2[...]
        adj = (jnp.concatenate([s2, s2], 1) * fields[k]).astype(BF16)
        bk = mm(adj, tb[B_BACK : B_BACK + 512]).astype(BF16)
        g = mm(tb[B_INVT : B_INVT + 256], bk)
        gre = g[:128, :128] + g[128:, 128:]
        gim = g[:128, 128:] - g[128:, :128]
        gacc[:, :128] += kr * gre + ki * gim
        gacc[:, 128:] += kr * gim - ki * gre
        return 0

    lax.fori_loop(0, KERNELS, back, 0)

    cc = remote(10, gacc, gother, s_corner, partner)
    cc.start()
    arrived(gother, s_corner)
    hbuf[1] = (gacc[...] + gother[...]).astype(BF16)
    hl = remote(11, hbuf.at[1], hbuf.at[2], s_spec.at[1], left)
    hr = remote(12, hbuf.at[1], hbuf.at[0], s_spec.at[0], right)

    @pl.when(has_l)
    def _():
        hl.start()

    @pl.when(has_r)
    def _():
        hr.start()

    glift[0:128] = mm(hbuf[1], ta[A_FWD : A_FWD + 256])
    glift[128:256] = mm(hbuf[1], ta[A_TURN : A_TURN + 256])

    rows0 = pl.multiple_of(128 + 128 * c, 128)
    below = pl.multiple_of(256 + 128 * c, 128)
    above = pl.multiple_of(112 + 128 * c, 16)
    lane = lax.broadcasted_iota(jnp.int32, (EXT, 128), 1)

    def level_rows(blk):
        main = win[blk, pl.ds(rows0, 128)].astype(F32)
        after = win[blk, pl.ds(below, 16)].astype(F32)[0:8]
        before = win[blk, pl.ds(above, 16)].astype(F32)[8:16]
        return jnp.concatenate([main, after, before], 0)

    def ring(x, y):
        return jnp.where(lane < 64, x, y)

    level = jnp.concatenate([level_rows(1), level_rows(2), ring(level_rows(3), level_rows(0))], 1)
    trans = jnp.tanh(0.25 * level)
    final[:, 0:LANES] = level
    final[:, LANES : 2 * LANES] = 0.25 * (1.0 - trans * trans)

    @pl.when(has_l)
    def _():
        arrived(hbuf.at[0], s_spec.at[0])

    @pl.when(has_r)
    def _():
        arrived(hbuf.at[2], s_spec.at[1])

    for r, q in ((0, A_FWD), (128, A_TURN)):
        glift[r : r + 128, 0:256] += mm(hbuf[0], ta[q : q + 256, 256:512])
        glift[r : r + 128, 256:512] += mm(hbuf[2], ta[q : q + 256, 0:256])
    gl = glift[...].astype(BF16)

    gblk = [glift[:, 128 * i : 128 * i + 128] for i in range(4)]
    out_l = jnp.where(has_l, gblk[0], gblk[1]).astype(BF16)
    out_r = jnp.where(has_r, gblk[3], gblk[2]).astype(BF16)
    strip = mm(tb[pl.ds(pl.multiple_of(B_STRIP + EXT * c, 16), EXT)], jnp.concatenate([out_l, out_r], 1))
    pick_l = one_hot((16, 128), [(0, 0), (1, 1), (2, 0), (3, 1)])
    pick_r = one_hot((16, 128), [(0, 126), (1, 127), (2, 126), (3, 127)])
    picked = jnp.concatenate([mm_nt(pick_l, gl[:, 128:256]), mm_nt(pick_r, gl[:, 256:384])], 0)
    crossed = mm(picked.astype(BF16), tb[pl.ds(pl.multiple_of(B_CROSS + 256 * c, 16), 256)])
    row16 = lax.broadcasted_iota(jnp.int32, (16, 128), 0)
    for side in range(2):
        cols = slice(128 * side, 128 * side + 128)
        cr = crossed[16 * side : 16 * side + 16]
        edge = jnp.where(row16 < 2, cr[:, :128], cr[:, 128:]).astype(BF16)
        part = strip[:, cols]
        msg_s[side, 0:16] = edge
        msg_s[side, 16:160] = part.astype(BF16)
        small_s[side, 0:16] = edge
        small_s[side, 16:32] = jnp.where(is0, part[128:144], part[16:32]).astype(BF16)

    ml = remote(13, msg_s.at[0], msg_r.at[1 - zl], s_msg.at[1 - zl], (ar, bl, c))
    mr = remote(14, msg_s.at[1], msg_r.at[zr], s_msg.at[zr], (ar, br, c))
    nl = remote(15, small_s.at[0], small_r.at[1 - zl], s_small.at[1 - zl], (ar, bl, other))
    nr = remote(16, small_s.at[1], small_r.at[zr], s_small.at[zr], (ar, br, other))

    @pl.when(send_ok)
    def _():
        ml.start()
        mr.start()
        nl.start()
        nr.start()

    ring_lane = lax.broadcasted_iota(jnp.int32, (256, 128), 1)
    gl_ring = jnp.where(ring_lane < 64, gblk[3], gblk[0]).astype(BF16)
    own_rows = tb[pl.ds(pl.multiple_of(B_OWN + EXT * c, 16), EXT)]
    grad = mm(own_rows, jnp.concatenate([gl[:, 128:384], gl_ring], 1))

    @pl.when(recv_ok)
    def _():
        arrived(msg_r.at[0], s_msg.at[0])
        arrived(msg_r.at[1], s_msg.at[1])

    @pl.when(small_ok)
    def _():
        arrived(small_r.at[0], s_small.at[0])
        arrived(small_r.at[1], s_small.at[1])

    eye = one_hot((128, 128), [])
    r128 = lax.broadcasted_iota(jnp.int32, (128, 128), 0)
    c128 = lax.broadcasted_iota(jnp.int32, (128, 128), 1)
    eye = jnp.where(r128 == c128, 1.0, 0.0).astype(BF16)
    sel_a = one_hot((32, 128), [(0, 126), (1, 127), (16, 0), (17, 1)])
    sel_b = one_hot((32, 128), [(2, 126), (3, 127), (18, 0), (19, 1)])
    edges = jnp.concatenate([msg_r[0, 0:16], msg_r[1, 0:16]], 0)
    edges_s = jnp.concatenate([small_r[0, 0:16], small_r[1, 0:16]], 0)
    turned = mm_nt(eye, edges).astype(BF16)
    turned_s = mm_nt(eye, edges_s).astype(BF16)
    col_main = mm(turned, sel_a)
    col_far = mm(turned, sel_b)
    col_small = mm(turned_s, sel_a)

    def add_part(blocks_main, blocks_ext, blocks_small):
        main = jnp.concatenate(blocks_main, 1)
        far = jnp.concatenate(blocks_ext, 1)
        near = jnp.concatenate(blocks_small, 1)
        after = jnp.where(is0, near[0:8], far[0:8])
        before = jnp.where(is0, far[8:16], near[8:16])
        return jnp.concatenate([main, after, before], 0)

    col_far16 = jnp.concatenate([col_far[0:8], col_far[120:128]], 0)
    col_small16 = jnp.concatenate([col_small[0:8], col_small[120:128]], 0)
    received = add_part(
        [msg_r[0, 32:160].astype(F32), msg_r[1, 32:160].astype(F32), col_main],
        [msg_r[0, 16:32].astype(F32), msg_r[1, 16:32].astype(F32), col_far16],
        [small_r[0, 16:32].astype(F32), small_r[1, 16:32].astype(F32), col_small16],
    )
    speed = SPEED_GAIN * (grad + received) * final[:, LANES : 2 * LANES]

    row = lax.broadcasted_iota(jnp.int32, (EXT, LANES), 0)
    col = lax.broadcasted_iota(jnp.int32, (EXT, LANES), 1)
    i_off = jnp.where(row < 136, row, row - EXT) + 128 * c
    j_off = jnp.where(col < 320, col, col - LANES)
    i_all = a * TILE + i_off
    j_all = b * TILE + j_off
    inside = (i_all >= 0) & (i_all < n_ty * TILE) & (j_all >= 0) & (j_all < n_tx * TILE)

    level = final[:, 0:LANES]
    for _ in range(LS_STEPS):
        up = pltpu.roll(level, 1, 0)
        down = pltpu.roll(level, EXT - 1, 0)
        lf = pltpu.roll(level, 1, 1)
        rt = pltpu.roll(level, LANES - 1, 1)
        sy = 0.5 * (down - up)
        sx = 0.5 * (rt - lf)
        spread = up + down + lf + rt - 4.0 * level
        level = level - speed * jnp.sqrt(GRAD_FLOOR + sy * sy + sx * sx) + SMOOTHING * spread
        level = jnp.where(inside, level, 0.0)
    final[0:128, 0:256] = level[0:128, 0:256]

    mine = out_hbm.at[pl.ds(pl.multiple_of(128 * c, 128), 128)]
    result = final.at[pl.ds(0, 128), pl.ds(0, 256)]
    ff = remote(17, result, mine, s_final, partner)
    ff.start()
    cp_out = local(result, mine, out_sem.at[1])

    cp_resist.wait()
    cp_out.wait()

    @pl.when(send_ok)
    def _():
        for d in (fl, fr, ml, mr, nl, nr):
            d.wait_send()

    @pl.when(has_l)
    def _():
        sl.wait_send()
        hl.wait_send()

    @pl.when(has_r)
    def _():
        sr.wait_send()
        hr.wait_send()

    @pl.when(recv_ok)
    def _():
        pl_.wait_send()
        pr_.wait_send()

    @pl.when(recv_ok & has_l)
    def _():
        fan_l[0].wait_send()
        fan_l[1].wait_send()

    @pl.when(recv_ok & has_r)
    def _():
        fan_r[0].wait_send()
        fan_r[1].wait_send()

    cc.wait_send()
    ff.wait_send()
    arrived(out_hbm.at[pl.ds(pl.multiple_of(128 * other, 128), 128)], s_final)


def make_body(n_ty, n_tx):
    def body(level_init, target, kernels, corner_doses):
        ta, tb = wide_tables()
        dma = pltpu.SemaphoreType.DMA
        anywhere = pl.BlockSpec(memory_space=pl.ANY)

        def whole(*args):
            return kernel(n_ty, n_tx, *args)

        return pl.pallas_call(
            whole,
            out_shape=(
                jax.ShapeDtypeStruct((1, TILE, TILE), F32),
                jax.ShapeDtypeStruct((TILE, TILE), F32),
            ),
            in_specs=[
                anywhere,
                anywhere,
                anywhere,
                pl.BlockSpec(memory_space=pltpu.SMEM),
                anywhere,
                anywhere,
            ],
            out_specs=(anywhere, anywhere),
            scratch_shapes=[
                pltpu.VMEM((TILE, TILE), jnp.int32),
                pltpu.VMEM((TILE, TILE), jnp.int32),
                pltpu.VMEM((1, KERNELS, 2, KF, KF), F32),
                pltpu.VMEM((A_ROWS, 512), BF16),
                pltpu.VMEM((B_ROWS, 256), BF16),
                pltpu.VMEM((4, WIN, 128), BF16),
                pltpu.VMEM((WIN, WIN), BF16),
                pltpu.VMEM((2, KF, KF), F32),
                pltpu.VMEM((KERNELS, TILE, 2 * TILE), F32),
                pltpu.VMEM((TILE, TILE), F32),
                pltpu.VMEM((TILE, TILE), F32),
                pltpu.VMEM((TILE, TILE), F32),
                pltpu.VMEM((KF, 2 * KF), F32),
                pltpu.VMEM((KF, 2 * KF), F32),
                pltpu.VMEM((3, KF, 2 * KF), BF16),
                pltpu.VMEM((2 * KF, WIN), F32),
                pltpu.VMEM((2 * KF, WIN), F32),
                pltpu.VMEM((2, 160, 128), BF16),
                pltpu.VMEM((2, 160, 128), BF16),
                pltpu.VMEM((2, 32, 128), BF16),
                pltpu.VMEM((2, 32, 128), BF16),
                pltpu.VMEM((EXT, 2 * LANES), F32),
                dma((5,)),
                dma((2,)),
                dma((18,)),
                dma((2,)),
                dma((2,)),
                dma((2, 2)),
                dma((2,)),
                dma,
                dma((2,)),
                dma((2,)),
                dma((2,)),
                dma,
            ],
            compiler_params=pltpu.CompilerParams(
                collective_id=0,
                has_side_effects=True,
                vmem_limit_bytes=62 * 1024 * 1024,
            ),
            cost_estimate=pl.CostEstimate(
                flops=1_500_000_000, bytes_accessed=6_000_000, transcendentals=400_000
            ),
        )(level_init, target, kernels, corner_doses, jnp.asarray(ta), jnp.asarray(tb))

    return body


def solution(mesh):
    in_specs = (P("ty", "tx"), P("ty", "tx"), P("corner", None, None, None, None), P("corner"))
    out_specs = (P("corner", "ty", "tx"), P("ty", "tx"))
    return jax.shard_map(
        make_body(mesh.shape["ty"], mesh.shape["tx"]),
        mesh=mesh,
        in_specs=in_specs,
        out_specs=out_specs,
        check_vma=False,
    )
```

```python
import math

import jax
import jax.numpy as jnp
import ml_dtypes
import numpy as np
from jax import lax
from jax.experimental import pallas as pl
from jax.experimental.pallas import tpu as pltpu
from jax.sharding import PartitionSpec as P

TILE = 256
HALO = 128
KF = 128
WIN = 512
KERNELS = 5
LS_STEPS = 3

STEEPNESS = 4.0
THRESHOLD = 1.0
SPEED_GAIN = 4.0
SMOOTHING = 0.24
GRAD_FLOOR = 0.25

MESH = pl.DeviceIdType.MESH
F32 = jnp.float32
BF16 = jnp.bfloat16

EXT = 144
LANES = 384


def wide_tables():
    shifts = np.arange(KF, dtype=np.int32) - KF // 2
    places = np.arange(WIN, dtype=np.int32)
    phases = (shifts[:, None] * places[None, :]) % WIN
    angles = np.float32(2.0 * math.pi / WIN) * phases.astype(np.float32)
    scaled = np.float32(1.0 / math.sqrt(WIN))
    fc = np.cos(angles, dtype=np.float32) * scaled
    fs = -np.sin(angles, dtype=np.float32) * scaled
    inner = angles[:, HALO : HALO + TILE].T
    ic = np.cos(inner, dtype=np.float32) * scaled
    isn = np.sin(inner, dtype=np.float32) * scaled
    fwd = np.concatenate([fc, fs], 0)
    turn = np.concatenate([-fs, fc], 0)
    to_field = np.concatenate(
        [np.concatenate([ic.T, isn.T], 1), np.concatenate([-isn.T, ic.T], 1)], 0
    )
    inv = np.concatenate([ic, isn], 1)
    ft = fwd.T
    lo, hi = HALO, HALO + 128
    own = [
        np.concatenate([ft[lo:hi], ft[hi : hi + 8], ft[lo - 8 : lo]], 0),
        np.concatenate([ft[hi : hi + 128], ft[hi + 128 : hi + 136], ft[hi - 8 : hi]], 0),
    ]
    strip = [ft[368:512], np.concatenate([ft[128:144], ft[0:128]], 0)]
    cross = [
        np.concatenate([fwd[:, 384:512], fwd[:, 256:384]], 1),
        fwd[:, 0:256],
    ]
    a = np.concatenate([fwd, turn, to_field], 0)
    b = np.concatenate([ft, inv, to_field.T, inv.T] + own + strip + cross, 0)
    return a.astype(ml_dtypes.bfloat16), b.astype(ml_dtypes.bfloat16)


A_FWD, A_TURN, A_FIELD, A_ROWS = 0, 256, 512, 768
B_FT, B_INV, B_BACK, B_INVT, B_OWN = 0, 512, 768, 1280, 1536
B_STRIP = B_OWN + 2 * EXT
B_CROSS = B_STRIP + 2 * EXT
B_ROWS = B_CROSS + 512


def mm(x, y):
    return jnp.dot(x, y, preferred_element_type=F32)


def mm_nt(x, y):
    return lax.dot_general(x, y, (((1,), (1,)), ((), ())), preferred_element_type=F32)


def one_hot(shape, pairs):
    rows = lax.broadcasted_iota(jnp.int32, shape, 0)
    cols = lax.broadcasted_iota(jnp.int32, shape, 1)
    hit = jnp.zeros(shape, F32)
    for r, c in pairs:
        hit = jnp.where((rows == r) & (cols == c), 1.0, hit)
    return hit.astype(BF16)


def kernel(
    n_ty,
    n_tx,
    level_hbm,
    target_hbm,
    kern_hbm,
    dose_ref,
    a_hbm,
    b_hbm,
    resist_hbm,
    out_hbm,
    level_i,
    target_i,
    kern,
    ta,
    tb,
    win,
    trw,
    spec,
    fields,
    inten,
    sens2,
    resist,
    gacc,
    gother,
    hbuf,
    lift,
    glift,
    msg_s,
    msg_r,
    small_s,
    small_r,
    final,
    held,
    in_sem,
    out_sem,
    send,
    s_side,
    s_far,
    s_fan,
    s_part,
    s_corner,
    s_spec,
    s_msg,
    s_small,
    s_final,
    s_held,
    ready,
    ready_relay,
):
    a, b, c = lax.axis_index("ty"), lax.axis_index("tx"), lax.axis_index("corner")
    has_l, has_r = b > 0, b < n_tx - 1
    up_ok, dn_ok = a > 0, a < n_ty - 1
    is0 = c == 0
    send_ok = jnp.where(is0, dn_ok.astype(jnp.int32), up_ok.astype(jnp.int32)) > 0
    recv_ok = jnp.where(is0, up_ok.astype(jnp.int32), dn_ok.astype(jnp.int32)) > 0
    ar = a + 1 - 2 * c
    bl, br = jnp.maximum(b - 1, 0), jnp.minimum(b + 1, n_tx - 1)
    zl, zr = jnp.where(has_l, 0, 1), jnp.where(has_r, 0, 1)
    other = 1 - c

    early_dn, early_up = (a % 8 == 3) & dn_ok, (a % 8 == 0) & up_ok
    late_up, late_dn = (a % 8 == 4) & up_ok, (a % 8 == 7) & dn_ok
    early, late = early_dn | early_up, late_up | late_dn
    far_row = jnp.where(early_dn | late_dn, a + 1, a - 1)
    far_core = jnp.where(early_dn | late_up, 0, 1)
    hops = early & (c == far_core)
    meets = late & (c == far_core)
    half = n_tx // 2
    bp = (b + half) % n_tx
    bpl, bpr = jnp.maximum(bp - 1, 0), jnp.minimum(bp + 1, n_tx - 1)
    zpl, zpr = jnp.where(bp > 0, 0, 1), jnp.where(bp < n_tx - 1, 0, 1)
    straight = send_ok & jnp.logical_not(hops)
    left, right, partner = (a, b - 1, c), (a, b + 1, c), (a, b, other)

    def local(src, dst, sem):
        cp = pltpu.make_async_copy(src, dst, sem)
        cp.start()
        return cp

    def remote(i, src, dst, rsem, dev):
        return pltpu.make_async_remote_copy(
            src_ref=src,
            dst_ref=dst,
            send_sem=send.at[i],
            recv_sem=rsem,
            device_id=dev,
            device_id_type=MESH,
        )

    def arrived(dst, rsem):
        pltpu.make_async_remote_copy(
            src_ref=dst,
            dst_ref=dst,
            send_sem=send.at[0],
            recv_sem=rsem,
            device_id=partner,
            device_id_type=MESH,
        ).wait_recv()

    cp_level = local(level_hbm, level_i, in_sem.at[0])
    cp_a = local(a_hbm, ta, in_sem.at[1])
    cp_kern = local(kern_hbm, kern, in_sem.at[2])
    cp_b = local(b_hbm, tb, in_sem.at[3])
    cp_target = local(target_hbm, target_i, in_sem.at[4])

    barrier = pltpu.get_barrier_semaphore()

    def hello(dev):
        pl.semaphore_signal(barrier, inc=1, device_id=dev, device_id_type=MESH)

    @pl.when(up_ok & jnp.logical_not(late_up))
    def _():
        hello((a - 1, bl, 0))
        hello((a - 1, br, 0))

    @pl.when(dn_ok & jnp.logical_not(late_dn))
    def _():
        hello((a + 1, bl, 1))
        hello((a + 1, br, 1))

    @pl.when(hops)
    def _():
        hello((a, bp, c))
        hello((far_row, bl, c))
        hello((far_row, br, c))
        hello((far_row, bpl, c))
        hello((far_row, bpr, c))

    hello(partner)

    @pl.when(has_l)
    def _():
        hello((a, b - 1, 0))
        hello((a, b - 1, 1))

    @pl.when(has_r)
    def _():
        hello((a, b + 1, 0))
        hello((a, b + 1, 1))

    cp_level.wait()
    level0 = level_i[...].astype(F32) * 0.125
    low = level0.astype(BF16)
    win[1, 128:384] = low[:, :128]
    win[2, 128:384] = low[:, 128:]

    wanted = (
        1
        + 2 * has_l.astype(jnp.int32)
        + 2 * has_r.astype(jnp.int32)
        + 4 * straight.astype(jnp.int32)
        + hops.astype(jnp.int32)
        + 4 * meets.astype(jnp.int32)
    )
    pl.semaphore_wait(barrier, wanted)

    @pl.when(late)
    def _():
        for to in (bl, br):
            pl.semaphore_signal(ready, inc=1, device_id=(far_row, to, far_core), device_id_type=MESH)

    @pl.when(meets)
    def _():
        for to in (bl, br):
            pl.semaphore_signal(
                ready_relay,
                inc=1,
                device_id=(far_row, (to + half) % n_tx, far_core),
                device_id_type=MESH,
            )

    srow = pl.multiple_of(256 - 128 * c, 128)
    hrow = pl.multiple_of(384 * c, 128)
    fl = remote(0, win.at[1, pl.ds(srow, 128)], win.at[jnp.where(has_l, 3, 1), pl.ds(hrow, 128)], s_far.at[1 - zl], (ar, bl, c))
    fr = remote(1, win.at[2, pl.ds(srow, 128)], win.at[jnp.where(has_r, 0, 2), pl.ds(hrow, 128)], s_far.at[zr], (ar, br, c))
    sl = remote(2, win.at[1, pl.ds(128, 256)], win.at[3, pl.ds(128, 256)], s_side.at[1], left)
    sr = remote(3, win.at[2, pl.ds(128, 256)], win.at[0, pl.ds(128, 256)], s_side.at[0], right)

    kl = remote(18, win.at[1, pl.ds(srow, 128)], held.at[0], s_held.at[0], (a, bp, c))
    kr_ = remote(19, win.at[2, pl.ds(srow, 128)], held.at[1], s_held.at[1], (a, bp, c))
    ol = remote(20, held.at[0], win.at[jnp.where(bp > 0, 3, 1), pl.ds(hrow, 128)], s_far.at[1 - zpl], (far_row, bpl, c))
    orr = remote(21, held.at[1], win.at[jnp.where(bp < n_tx - 1, 0, 2), pl.ds(hrow, 128)], s_far.at[zpr], (far_row, bpr, c))

    @pl.when(straight)
    def _():
        fl.start()
        fr.start()

    @pl.when(hops)
    def _():
        kl.start()
        kr_.start()

    @pl.when(has_l)
    def _():
        sl.start()

    @pl.when(has_r)
    def _():
        sr.start()

    @pl.when(jnp.logical_not(has_l))
    def _():
        win[0] = jnp.zeros((WIN, 128), BF16)
        hbuf[0] = jnp.zeros((KF, 256), BF16)

    @pl.when(jnp.logical_not(has_r))
    def _():
        win[3] = jnp.zeros((WIN, 128), BF16)
        hbuf[2] = jnp.zeros((KF, 256), BF16)

    for q, ok in ((0, up_ok), (384, dn_ok)):
        @pl.when(jnp.logical_not(ok))
        def _(q=q):
            for blk in range(4):
                win[blk, q : q + 128] = jnp.zeros((128, 128), BF16)

    @pl.when(jnp.logical_not(recv_ok))
    def _():
        msg_r[...] = jnp.zeros_like(msg_r)

    small_ok = jnp.where(is0, dn_ok.astype(jnp.int32), up_ok.astype(jnp.int32)) > 0

    @pl.when(jnp.logical_not(small_ok))
    def _():
        small_r[...] = jnp.zeros_like(small_r)

    def to_trans(blk, r0, rows):
        x = win[blk, r0 : r0 + rows].astype(F32)
        trw[r0 : r0 + rows, blk * 128 : blk * 128 + 128] = jnp.tanh(0.25 * x).astype(BF16)

    to_trans(1, 128, 256)
    to_trans(2, 128, 256)

    @pl.when(has_l)
    def _():
        arrived(win.at[0, pl.ds(128, 256)], s_side.at[0])

    to_trans(0, 128, 256)

    @pl.when(has_r)
    def _():
        arrived(win.at[3, pl.ds(128, 256)], s_side.at[1])

    to_trans(3, 128, 256)
    cp_a.wait()
    cp_b.wait()
    cp_kern.wait()
    cp_target.wait()
    lift[...] = mm(ta[A_FWD : A_FWD + 256, 128:384], trw[128:384, :])

    @pl.when(hops)
    def _():
        pl.semaphore_wait(ready_relay, 2)
        arrived(held.at[0], s_held.at[0])
        ol.start()
        arrived(held.at[1], s_held.at[1])
        orr.start()

    blk_l, blk_r = jnp.where(has_l, 0, 1), jnp.where(has_r, 3, 2)
    got_l, got_r = win.at[blk_l, pl.ds(hrow, 128)], win.at[blk_r, pl.ds(hrow, 128)]
    pl_ = remote(4, got_l, got_l, s_part.at[0], partner)
    pr_ = remote(5, got_r, got_r, s_part.at[1], partner)
    fan_l = [remote(6 + d, got_l, win.at[2, pl.ds(hrow, 128)], s_fan.at[c, 1], (a, b - 1, d)) for d in (0, 1)]
    fan_r = [remote(8 + d, got_r, win.at[1, pl.ds(hrow, 128)], s_fan.at[c, 0], (a, b + 1, d)) for d in (0, 1)]

    @pl.when(recv_ok)
    def _():
        arrived(got_l, s_far.at[0])

        @pl.when(has_l)
        def _():
            fan_l[0].start()
            fan_l[1].start()

        pl_.start()
        arrived(got_r, s_far.at[1])

        @pl.when(has_r)
        def _():
            fan_r[0].start()
            fan_r[1].start()

        pr_.start()

    @pl.when(small_ok)
    def _():
        orow = pl.multiple_of(384 * other, 128)
        arrived(win.at[blk_l, pl.ds(orow, 128)], s_part.at[0])
        arrived(win.at[blk_r, pl.ds(orow, 128)], s_part.at[1])

    for d, ok in ((0, up_ok), (1, dn_ok)):
        @pl.when(ok & has_l)
        def _(d=d):
            arrived(win.at[1, pl.ds(384 * d, 128)], s_fan.at[d, 0])

        @pl.when(ok & has_r)
        def _(d=d):
            arrived(win.at[2, pl.ds(384 * d, 128)], s_fan.at[d, 1])

    for blk in range(4):
        to_trans(blk, 0, 128)
        to_trans(blk, 384, 128)
    lift_b = (
        lift[...]
        + mm(ta[A_FWD : A_FWD + 256, 0:128], trw[0:128, :])
        + mm(ta[A_FWD : A_FWD + 256, 384:512], trw[384:512, :])
    ).astype(BF16)
    s = mm(lift_b, tb[B_FT : B_FT + 512])
    spec[0] = s[:128, :128] - s[128:, 128:]
    spec[1] = s[:128, 128:] + s[128:, :128]

    dose = dose_ref[0]
    inten[...] = jnp.zeros_like(inten)

    def ahead(k, _):
        kr, ki = kern[0, k, 0], kern[0, k, 1]
        sre, sim = spec[0], spec[1]
        bre = (kr * sre - ki * sim).astype(BF16)
        bim = (kr * sim + ki * sre).astype(BF16)
        blur = jnp.concatenate(
            [jnp.concatenate([bre, bim], 1), jnp.concatenate([-bim, bre], 1)], 0
        )
        proj = mm(tb[B_INV : B_INV + 256], blur).astype(BF16)
        field = mm(proj, ta[A_FIELD : A_FIELD + 256])
        fields[k] = field
        fre, fim = field[:, :256], field[:, 256:]
        inten[...] += fre * fre + fim * fim
        return 0

    lax.fori_loop(0, KERNELS, ahead, 0)

    res = jax.nn.sigmoid(STEEPNESS * (dose * inten[...] - THRESHOLD))
    resist[...] = res
    cp_resist = local(resist, resist_hbm.at[0], out_sem.at[0])
    goal = target_i[...].astype(F32)
    sens2[...] = 2.0 * (2.0 * (res - goal) * STEEPNESS * dose * res * (1.0 - res))
    gacc[...] = jnp.zeros_like(gacc)

    def back(k, _):
        kr, ki = kern[0, k, 0], kern[0, k, 1]
        s2 = sens2[...]
        adj = (jnp.concatenate([s2, s2], 1) * fields[k]).astype(BF16)
        bk = mm(adj, tb[B_BACK : B_BACK + 512]).astype(BF16)
        g = mm(tb[B_INVT : B_INVT + 256], bk)
        gre = g[:128, :128] + g[128:, 128:]
        gim = g[:128, 128:] - g[128:, :128]
        gacc[:, :128] += kr * gre + ki * gim
        gacc[:, 128:] += kr * gim - ki * gre
        return 0

    lax.fori_loop(0, KERNELS, back, 0)

    cc = remote(10, gacc, gother, s_corner, partner)
    cc.start()
    arrived(gother, s_corner)
    hbuf[1] = (gacc[...] + gother[...]).astype(BF16)
    hl = remote(11, hbuf.at[1], hbuf.at[2], s_spec.at[1], left)
    hr = remote(12, hbuf.at[1], hbuf.at[0], s_spec.at[0], right)

    @pl.when(has_l)
    def _():
        hl.start()

    @pl.when(has_r)
    def _():
        hr.start()

    glift[0:128] = mm(hbuf[1], ta[A_FWD : A_FWD + 256])
    glift[128:256] = mm(hbuf[1], ta[A_TURN : A_TURN + 256])

    rows0 = pl.multiple_of(128 + 128 * c, 128)
    below = pl.multiple_of(256 + 128 * c, 128)
    above = pl.multiple_of(112 + 128 * c, 16)
    lane = lax.broadcasted_iota(jnp.int32, (EXT, 128), 1)

    def level_rows(blk):
        main = win[blk, pl.ds(rows0, 128)].astype(F32)
        after = win[blk, pl.ds(below, 16)].astype(F32)[0:8]
        before = win[blk, pl.ds(above, 16)].astype(F32)[8:16]
        return jnp.concatenate([main, after, before], 0)

    def ring(x, y):
        return jnp.where(lane < 64, x, y)

    level = jnp.concatenate([level_rows(1), level_rows(2), ring(level_rows(3), level_rows(0))], 1)
    trans = jnp.tanh(0.25 * level)
    final[:, 0:LANES] = level
    final[:, LANES : 2 * LANES] = 0.25 * (1.0 - trans * trans)

    @pl.when(has_l)
    def _():
        arrived(hbuf.at[0], s_spec.at[0])

    @pl.when(has_r)
    def _():
        arrived(hbuf.at[2], s_spec.at[1])

    for r, q in ((0, A_FWD), (128, A_TURN)):
        glift[r : r + 128, 0:256] += mm(hbuf[0], ta[q : q + 256, 256:512])
        glift[r : r + 128, 256:512] += mm(hbuf[2], ta[q : q + 256, 0:256])
    gl = glift[...].astype(BF16)

    gblk = [glift[:, 128 * i : 128 * i + 128] for i in range(4)]
    out_l = jnp.where(has_l, gblk[0], gblk[1]).astype(BF16)
    out_r = jnp.where(has_r, gblk[3], gblk[2]).astype(BF16)
    strip = mm(tb[pl.ds(pl.multiple_of(B_STRIP + EXT * c, 16), EXT)], jnp.concatenate([out_l, out_r], 1))
    pick_l = one_hot((16, 128), [(0, 0), (1, 1), (2, 0), (3, 1)])
    pick_r = one_hot((16, 128), [(0, 126), (1, 127), (2, 126), (3, 127)])
    picked = jnp.concatenate([mm_nt(pick_l, gl[:, 128:256]), mm_nt(pick_r, gl[:, 256:384])], 0)
    crossed = mm(picked.astype(BF16), tb[pl.ds(pl.multiple_of(B_CROSS + 256 * c, 16), 256)])
    row16 = lax.broadcasted_iota(jnp.int32, (16, 128), 0)
    for side in range(2):
        cols = slice(128 * side, 128 * side + 128)
        cr = crossed[16 * side : 16 * side + 16]
        edge = jnp.where(row16 < 2, cr[:, :128], cr[:, 128:])[0:8]
        part = strip[:, cols]
        near_rows = jnp.where(is0, part[8:16], part[0:8])
        msg_s[side, 0:16] = jnp.concatenate([edge, near_rows], 0).astype(BF16)
        msg_s[side, 16:EXT] = part[16:EXT].astype(BF16)
        tail_rows = jnp.where(is0, part[136:144], part[16:24])
        small_s[side] = jnp.concatenate([edge, tail_rows], 0).astype(BF16)

    ml = remote(13, msg_s.at[0], msg_r.at[1 - zl], s_msg.at[1 - zl], (ar, bl, c))
    mr = remote(14, msg_s.at[1], msg_r.at[zr], s_msg.at[zr], (ar, br, c))
    nl = remote(15, small_s.at[0], small_r.at[1 - zl], s_small.at[1 - zl], (ar, bl, other))
    nr = remote(16, small_s.at[1], small_r.at[zr], s_small.at[zr], (ar, br, other))

    @pl.when(hops)
    def _():
        pl.semaphore_wait(ready, 4)

    @pl.when(send_ok)
    def _():
        ml.start()
        mr.start()
        nl.start()
        nr.start()

    ring_lane = lax.broadcasted_iota(jnp.int32, (256, 128), 1)
    gl_ring = jnp.where(ring_lane < 64, gblk[3], gblk[0]).astype(BF16)
    own_rows = tb[pl.ds(pl.multiple_of(B_OWN + EXT * c, 16), EXT)]
    grad = mm(own_rows, jnp.concatenate([gl[:, 128:384], gl_ring], 1))

    @pl.when(recv_ok)
    def _():
        arrived(msg_r.at[0], s_msg.at[0])
        arrived(msg_r.at[1], s_msg.at[1])

    @pl.when(small_ok)
    def _():
        arrived(small_r.at[0], s_small.at[0])
        arrived(small_r.at[1], s_small.at[1])

    eye = one_hot((128, 128), [])
    r128 = lax.broadcasted_iota(jnp.int32, (128, 128), 0)
    c128 = lax.broadcasted_iota(jnp.int32, (128, 128), 1)
    eye = jnp.where(r128 == c128, 1.0, 0.0).astype(BF16)
    sel_a = one_hot((32, 128), [(0, 126), (1, 127), (16, 0), (17, 1)])
    sel_b = one_hot((32, 128), [(2, 126), (3, 127), (18, 0), (19, 1)])
    edges = jnp.concatenate([msg_r[0, 0:16], msg_r[1, 0:16]], 0)
    edges_s = jnp.concatenate([small_r[0], small_r[1]], 0)
    turned = mm_nt(eye, edges).astype(BF16)
    turned_s = mm_nt(eye, edges_s).astype(BF16)
    col_main = mm(turned, sel_a)
    col_far = mm(turned, sel_b)
    col_small = mm(turned_s, sel_a)

    def add_part(blocks_main, blocks_ext, blocks_small):
        main = jnp.concatenate(blocks_main, 1)
        far = jnp.concatenate(blocks_ext, 1)
        near = jnp.concatenate(blocks_small, 1)
        after = jnp.where(is0, near[0:8], far[0:8])
        before = jnp.where(is0, far[8:16], near[8:16])
        return jnp.concatenate([main, after, before], 0)

    def twice(x):
        rows = x.astype(F32)[8:16]
        return jnp.concatenate([rows, rows], 0)

    col_far16 = jnp.concatenate([col_far[0:8], col_far[120:128]], 0)
    col_small16 = jnp.concatenate([col_small[0:8], col_small[120:128]], 0)
    received = add_part(
        [msg_r[0, 16:EXT].astype(F32), msg_r[1, 16:EXT].astype(F32), col_main],
        [twice(msg_r[0, 0:16]), twice(msg_r[1, 0:16]), col_far16],
        [twice(small_r[0]), twice(small_r[1]), col_small16],
    )
    speed = SPEED_GAIN * (grad + received) * final[:, LANES : 2 * LANES]

    row = lax.broadcasted_iota(jnp.int32, (EXT, LANES), 0)
    col = lax.broadcasted_iota(jnp.int32, (EXT, LANES), 1)
    i_off = jnp.where(row < 136, row, row - EXT) + 128 * c
    j_off = jnp.where(col < 320, col, col - LANES)
    i_all = a * TILE + i_off
    j_all = b * TILE + j_off
    inside = (i_all >= 0) & (i_all < n_ty * TILE) & (j_all >= 0) & (j_all < n_tx * TILE)

    level = final[:, 0:LANES]
    for _ in range(LS_STEPS):
        up = pltpu.roll(level, 1, 0)
        down = pltpu.roll(level, EXT - 1, 0)
        lf = pltpu.roll(level, 1, 1)
        rt = pltpu.roll(level, LANES - 1, 1)
        sy = 0.5 * (down - up)
        sx = 0.5 * (rt - lf)
        spread = up + down + lf + rt - 4.0 * level
        level = level - speed * jnp.sqrt(GRAD_FLOOR + sy * sy + sx * sx) + SMOOTHING * spread
        level = jnp.where(inside, level, 0.0)
    final[0:128, 0:256] = level[0:128, 0:256]

    mine = out_hbm.at[pl.ds(pl.multiple_of(128 * c, 128), 128)]
    result = final.at[pl.ds(0, 128), pl.ds(0, 256)]
    ff = remote(17, result, mine, s_final, partner)
    ff.start()
    cp_out = local(result, mine, out_sem.at[1])

    cp_resist.wait()
    cp_out.wait()

    @pl.when(straight)
    def _():
        fl.wait_send()
        fr.wait_send()

    @pl.when(hops)
    def _():
        for d in (kl, kr_, ol, orr):
            d.wait_send()

    @pl.when(send_ok)
    def _():
        for d in (ml, mr, nl, nr):
            d.wait_send()

    @pl.when(has_l)
    def _():
        sl.wait_send()
        hl.wait_send()

    @pl.when(has_r)
    def _():
        sr.wait_send()
        hr.wait_send()

    @pl.when(recv_ok)
    def _():
        pl_.wait_send()
        pr_.wait_send()

    @pl.when(recv_ok & has_l)
    def _():
        fan_l[0].wait_send()
        fan_l[1].wait_send()

    @pl.when(recv_ok & has_r)
    def _():
        fan_r[0].wait_send()
        fan_r[1].wait_send()

    cc.wait_send()
    ff.wait_send()
    arrived(out_hbm.at[pl.ds(pl.multiple_of(128 * other, 128), 128)], s_final)


def make_body(n_ty, n_tx):
    def body(level_init, target, kernels, corner_doses):
        ta, tb = wide_tables()
        dma = pltpu.SemaphoreType.DMA
        anywhere = pl.BlockSpec(memory_space=pl.ANY)

        def whole(*args):
            return kernel(n_ty, n_tx, *args)

        return pl.pallas_call(
            whole,
            out_shape=(
                jax.ShapeDtypeStruct((1, TILE, TILE), F32),
                jax.ShapeDtypeStruct((TILE, TILE), F32),
            ),
            in_specs=[
                anywhere,
                anywhere,
                anywhere,
                pl.BlockSpec(memory_space=pltpu.SMEM),
                anywhere,
                anywhere,
            ],
            out_specs=(anywhere, anywhere),
            scratch_shapes=[
                pltpu.VMEM((TILE, TILE), jnp.int32),
                pltpu.VMEM((TILE, TILE), jnp.int32),
                pltpu.VMEM((1, KERNELS, 2, KF, KF), F32),
                pltpu.VMEM((A_ROWS, 512), BF16),
                pltpu.VMEM((B_ROWS, 256), BF16),
                pltpu.VMEM((4, WIN, 128), BF16),
                pltpu.VMEM((WIN, WIN), BF16),
                pltpu.VMEM((2, KF, KF), F32),
                pltpu.VMEM((KERNELS, TILE, 2 * TILE), F32),
                pltpu.VMEM((TILE, TILE), F32),
                pltpu.VMEM((TILE, TILE), F32),
                pltpu.VMEM((TILE, TILE), F32),
                pltpu.VMEM((KF, 2 * KF), F32),
                pltpu.VMEM((KF, 2 * KF), F32),
                pltpu.VMEM((3, KF, 2 * KF), BF16),
                pltpu.VMEM((2 * KF, WIN), F32),
                pltpu.VMEM((2 * KF, WIN), F32),
                pltpu.VMEM((2, EXT, 128), BF16),
                pltpu.VMEM((2, EXT, 128), BF16),
                pltpu.VMEM((2, 16, 128), BF16),
                pltpu.VMEM((2, 16, 128), BF16),
                pltpu.VMEM((EXT, 2 * LANES), F32),
                pltpu.VMEM((2, 128, 128), BF16),
                dma((5,)),
                dma((2,)),
                dma((22,)),
                dma((2,)),
                dma((2,)),
                dma((2, 2)),
                dma((2,)),
                dma,
                dma((2,)),
                dma((2,)),
                dma((2,)),
                dma,
                dma((2,)),
                pltpu.SemaphoreType.REGULAR,
                pltpu.SemaphoreType.REGULAR,
            ],
            compiler_params=pltpu.CompilerParams(
                collective_id=0,
                has_side_effects=True,
                vmem_limit_bytes=54600 * 1024,
            ),
            cost_estimate=pl.CostEstimate(
                flops=1_500_000_000, bytes_accessed=6_000_000, transcendentals=400_000
            ),
        )(level_init, target, kernels, corner_doses, jnp.asarray(ta), jnp.asarray(tb))

    return body


def solution(mesh):
    in_specs = (P("ty", "tx"), P("ty", "tx"), P("corner", None, None, None, None), P("corner"))
    out_specs = (P("corner", "ty", "tx"), P("ty", "tx"))
    return jax.shard_map(
        make_body(mesh.shape["ty"], mesh.shape["tx"]),
        mesh=mesh,
        in_specs=in_specs,
        out_specs=out_specs,
        check_vma=False,
    )
```

```python
import math

import jax
import jax.numpy as jnp
import ml_dtypes
import numpy as np
from jax import lax
from jax.experimental import pallas as pl
from jax.experimental.pallas import tpu as pltpu
from jax.sharding import PartitionSpec as P

TILE = 256
HALO = 128
KF = 128
WIN = 512
KERNELS = 5
LS_STEPS = 3

STEEPNESS = 4.0
THRESHOLD = 1.0
SPEED_GAIN = 4.0
SMOOTHING = 0.24
GRAD_FLOOR = 0.25

MESH = pl.DeviceIdType.MESH
F32 = jnp.float32
BF16 = jnp.bfloat16

EXT = 144
LANES = 384


def wide_tables():
    shifts = np.arange(KF, dtype=np.int32) - KF // 2
    places = np.arange(WIN, dtype=np.int32)
    phases = (shifts[:, None] * places[None, :]) % WIN
    angles = np.float32(2.0 * math.pi / WIN) * phases.astype(np.float32)
    scaled = np.float32(1.0 / math.sqrt(WIN))
    fc = np.cos(angles, dtype=np.float32) * scaled
    fs = -np.sin(angles, dtype=np.float32) * scaled
    inner = angles[:, HALO : HALO + TILE].T
    ic = np.cos(inner, dtype=np.float32) * scaled
    isn = np.sin(inner, dtype=np.float32) * scaled
    fwd = np.concatenate([fc, fs], 0)
    turn = np.concatenate([-fs, fc], 0)
    to_field = np.concatenate(
        [np.concatenate([ic.T, isn.T], 1), np.concatenate([-isn.T, ic.T], 1)], 0
    )
    inv = np.concatenate([ic, isn], 1)
    ft = fwd.T
    lo, hi = HALO, HALO + 128
    own = [
        np.concatenate([ft[lo:hi], ft[hi : hi + 8], ft[lo - 8 : lo]], 0),
        np.concatenate([ft[hi : hi + 128], ft[hi + 128 : hi + 136], ft[hi - 8 : hi]], 0),
    ]
    strip = [ft[368:512], np.concatenate([ft[128:144], ft[0:128]], 0)]
    cross = [
        np.concatenate([fwd[:, 384:512], fwd[:, 256:384]], 1),
        fwd[:, 0:256],
    ]
    a = np.concatenate([fwd, turn, to_field], 0)
    b = np.concatenate([ft, inv, to_field.T, inv.T] + own + strip + cross, 0)
    return a.astype(ml_dtypes.bfloat16), b.astype(ml_dtypes.bfloat16)


A_FWD, A_TURN, A_FIELD, A_ROWS = 0, 256, 512, 768
B_FT, B_INV, B_BACK, B_INVT, B_OWN = 0, 512, 768, 1280, 1536
B_STRIP = B_OWN + 2 * EXT
B_CROSS = B_STRIP + 2 * EXT
B_ROWS = B_CROSS + 512


def mm(x, y):
    return jnp.dot(x, y, preferred_element_type=F32)


def mm_nt(x, y):
    return lax.dot_general(x, y, (((1,), (1,)), ((), ())), preferred_element_type=F32)


def one_hot(shape, pairs):
    rows = lax.broadcasted_iota(jnp.int32, shape, 0)
    cols = lax.broadcasted_iota(jnp.int32, shape, 1)
    hit = jnp.zeros(shape, F32)
    for r, c in pairs:
        hit = jnp.where((rows == r) & (cols == c), 1.0, hit)
    return hit.astype(BF16)


def kernel(
    n_ty,
    n_tx,
    level_hbm,
    target_hbm,
    kern_hbm,
    dose_ref,
    a_hbm,
    b_hbm,
    resist_hbm,
    out_hbm,
    level_i,
    target_i,
    kern,
    ta,
    tb,
    win,
    trw,
    spec,
    fields,
    proj,
    inten,
    sens2,
    resist,
    gacc,
    gother,
    hbuf,
    lift,
    glift,
    msg_s,
    msg_r,
    small_s,
    small_r,
    final,
    held,
    in_sem,
    out_sem,
    send,
    s_side,
    s_far,
    s_fan,
    s_part,
    s_corner,
    s_spec,
    s_msg,
    s_small,
    s_final,
    s_held,
    ready,
    ready_relay,
):
    a, b, c = lax.axis_index("ty"), lax.axis_index("tx"), lax.axis_index("corner")
    has_l, has_r = b > 0, b < n_tx - 1
    up_ok, dn_ok = a > 0, a < n_ty - 1
    is0 = c == 0
    send_ok = jnp.where(is0, dn_ok.astype(jnp.int32), up_ok.astype(jnp.int32)) > 0
    recv_ok = jnp.where(is0, up_ok.astype(jnp.int32), dn_ok.astype(jnp.int32)) > 0
    ar = a + 1 - 2 * c
    bl, br = jnp.maximum(b - 1, 0), jnp.minimum(b + 1, n_tx - 1)
    zl, zr = jnp.where(has_l, 0, 1), jnp.where(has_r, 0, 1)
    other = 1 - c

    early_dn, early_up = (a % 8 == 3) & dn_ok, (a % 8 == 0) & up_ok
    late_up, late_dn = (a % 8 == 4) & up_ok, (a % 8 == 7) & dn_ok
    early, late = early_dn | early_up, late_up | late_dn
    far_row = jnp.where(early_dn | late_dn, a + 1, a - 1)
    far_core = jnp.where(early_dn | late_up, 0, 1)
    hops = early & (c == far_core)
    meets = late & (c == far_core)
    half = n_tx // 2
    bp = (b + half) % n_tx
    bpl, bpr = jnp.maximum(bp - 1, 0), jnp.minimum(bp + 1, n_tx - 1)
    zpl, zpr = jnp.where(bp > 0, 0, 1), jnp.where(bp < n_tx - 1, 0, 1)
    straight = send_ok & jnp.logical_not(hops)
    left, right, partner = (a, b - 1, c), (a, b + 1, c), (a, b, other)

    def local(src, dst, sem):
        cp = pltpu.make_async_copy(src, dst, sem)
        cp.start()
        return cp

    def remote(i, src, dst, rsem, dev):
        return pltpu.make_async_remote_copy(
            src_ref=src,
            dst_ref=dst,
            send_sem=send.at[i],
            recv_sem=rsem,
            device_id=dev,
            device_id_type=MESH,
        )

    def arrived(dst, rsem):
        pltpu.make_async_remote_copy(
            src_ref=dst,
            dst_ref=dst,
            send_sem=send.at[0],
            recv_sem=rsem,
            device_id=partner,
            device_id_type=MESH,
        ).wait_recv()

    started = []

    def start(cond, *copies):
        started.append((cond, copies))

        @pl.when(cond)
        def _():
            for d in copies:
                d.start()

    def settle():
        for cond, copies in started:

            @pl.when(cond)
            def _(copies=copies):
                for d in copies:
                    d.wait_send()

    cp_level = local(level_hbm, level_i, in_sem.at[0])
    cp_a = local(a_hbm, ta, in_sem.at[1])
    cp_kern = local(kern_hbm, kern, in_sem.at[2])
    cp_b = local(b_hbm, tb, in_sem.at[3])
    cp_target = local(target_hbm, target_i, in_sem.at[4])

    barrier = pltpu.get_barrier_semaphore()

    def hello(dev):
        pl.semaphore_signal(barrier, inc=1, device_id=dev, device_id_type=MESH)

    @pl.when(up_ok & jnp.logical_not(late_up))
    def _():
        hello((a - 1, bl, 0))
        hello((a - 1, br, 0))

    @pl.when(dn_ok & jnp.logical_not(late_dn))
    def _():
        hello((a + 1, bl, 1))
        hello((a + 1, br, 1))

    @pl.when(hops)
    def _():
        hello((a, bp, c))
        hello((far_row, bl, c))
        hello((far_row, br, c))
        hello((far_row, bpl, c))
        hello((far_row, bpr, c))

    hello(partner)

    @pl.when(has_l)
    def _():
        hello((a, b - 1, 0))
        hello((a, b - 1, 1))

    @pl.when(has_r)
    def _():
        hello((a, b + 1, 0))
        hello((a, b + 1, 1))

    cp_level.wait()
    level0 = level_i[...].astype(F32) * 0.125
    low = level0.astype(BF16)
    win[1, 128:384] = low[:, :128]
    win[2, 128:384] = low[:, 128:]

    wanted = (
        1
        + 2 * has_l.astype(jnp.int32)
        + 2 * has_r.astype(jnp.int32)
        + 4 * straight.astype(jnp.int32)
        + hops.astype(jnp.int32)
        + 4 * meets.astype(jnp.int32)
    )
    pl.semaphore_wait(barrier, wanted)

    @pl.when(late)
    def _():
        for to in (bl, br):
            pl.semaphore_signal(ready, inc=1, device_id=(far_row, to, far_core), device_id_type=MESH)

    @pl.when(meets)
    def _():
        for to in (bl, br):
            pl.semaphore_signal(
                ready_relay,
                inc=1,
                device_id=(far_row, (to + half) % n_tx, far_core),
                device_id_type=MESH,
            )

    srow = pl.multiple_of(256 - 128 * c, 128)
    hrow = pl.multiple_of(384 * c, 128)
    fl = remote(0, win.at[1, pl.ds(srow, 128)], win.at[jnp.where(has_l, 3, 1), pl.ds(hrow, 128)], s_far.at[1 - zl], (ar, bl, c))
    fr = remote(1, win.at[2, pl.ds(srow, 128)], win.at[jnp.where(has_r, 0, 2), pl.ds(hrow, 128)], s_far.at[zr], (ar, br, c))
    sl = remote(2, win.at[1, pl.ds(128, 256)], win.at[3, pl.ds(128, 256)], s_side.at[1], left)
    sr = remote(3, win.at[2, pl.ds(128, 256)], win.at[0, pl.ds(128, 256)], s_side.at[0], right)

    kl = remote(24, win.at[1, pl.ds(srow, 128)], held.at[0], s_held.at[0], (a, bp, c))
    kr_ = remote(25, win.at[2, pl.ds(srow, 128)], held.at[1], s_held.at[1], (a, bp, c))
    ol = remote(26, held.at[0], win.at[jnp.where(bp > 0, 3, 1), pl.ds(hrow, 128)], s_far.at[1 - zpl], (far_row, bpl, c))
    orr = remote(27, held.at[1], win.at[jnp.where(bp < n_tx - 1, 0, 2), pl.ds(hrow, 128)], s_far.at[zpr], (far_row, bpr, c))

    start(hops, kl, kr_)
    start(straight, fl, fr)
    start(has_l, sl)
    start(has_r, sr)

    @pl.when(jnp.logical_not(has_l))
    def _():
        win[0] = jnp.zeros((WIN, 128), BF16)
        hbuf[0] = jnp.zeros((KF, 256), BF16)

    @pl.when(jnp.logical_not(has_r))
    def _():
        win[3] = jnp.zeros((WIN, 128), BF16)
        hbuf[2] = jnp.zeros((KF, 256), BF16)

    for q, ok in ((0, up_ok), (384, dn_ok)):
        @pl.when(jnp.logical_not(ok))
        def _(q=q):
            for blk in range(4):
                win[blk, q : q + 128] = jnp.zeros((128, 128), BF16)

    @pl.when(jnp.logical_not(recv_ok))
    def _():
        msg_r[...] = jnp.zeros_like(msg_r)

    small_ok = jnp.where(is0, dn_ok.astype(jnp.int32), up_ok.astype(jnp.int32)) > 0

    @pl.when(jnp.logical_not(small_ok))
    def _():
        small_r[...] = jnp.zeros_like(small_r)

    def to_trans(blk, r0, rows):
        x = win[blk, r0 : r0 + rows].astype(F32)
        trw[r0 : r0 + rows, blk * 128 : blk * 128 + 128] = jnp.tanh(0.25 * x).astype(BF16)

    to_trans(1, 128, 256)
    to_trans(2, 128, 256)

    @pl.when(has_l)
    def _():
        arrived(win.at[0, pl.ds(128, 256)], s_side.at[0])

    to_trans(0, 128, 256)

    @pl.when(has_r)
    def _():
        arrived(win.at[3, pl.ds(128, 256)], s_side.at[1])

    to_trans(3, 128, 256)
    cp_a.wait()
    cp_b.wait()
    cp_kern.wait()
    cp_target.wait()
    lift[...] = mm(ta[A_FWD : A_FWD + 256, 128:384], trw[128:384, :])

    @pl.when(hops)
    def _():
        pl.semaphore_wait(ready_relay, 2)
        arrived(held.at[0], s_held.at[0])
        ol.start()
        arrived(held.at[1], s_held.at[1])
        orr.start()

    started.append((hops, (ol, orr)))

    blk_l, blk_r = jnp.where(has_l, 0, 1), jnp.where(has_r, 3, 2)
    first = jnp.where(late_up | early_up, 1, jnp.where(late_dn | early_dn, 0, c))
    for step in range(2):
        d = first if step == 0 else 1 - first
        ok = jnp.where(d == 0, up_ok.astype(jnp.int32), dn_ok.astype(jnp.int32)) > 0
        mine, theirs = ok & (d == c), ok & (d != c)
        hr_ = pl.multiple_of(384 * d, 128)
        got_l, got_r = win.at[blk_l, pl.ds(hr_, 128)], win.at[blk_r, pl.ds(hr_, 128)]
        n0 = 4 + 6 * step
        part_l = remote(n0, got_l, got_l, s_part.at[0], partner)
        part_r = remote(n0 + 1, got_r, got_r, s_part.at[1], partner)
        fan_l = [
            remote(n0 + 2 + e, got_l, win.at[2, pl.ds(hr_, 128)], s_fan.at[d, 1], (a, b - 1, e))
            for e in (0, 1)
        ]
        fan_r = [
            remote(n0 + 4 + e, got_r, win.at[1, pl.ds(hr_, 128)], s_fan.at[d, 0], (a, b + 1, e))
            for e in (0, 1)
        ]

        @pl.when(mine)
        def _(got=got_l):
            arrived(got, s_far.at[0])

        start(mine & has_l, *fan_l)
        start(mine, part_l)

        @pl.when(mine)
        def _(got=got_r):
            arrived(got, s_far.at[1])

        start(mine & has_r, *fan_r)
        start(mine, part_r)

        @pl.when(theirs)
        def _(got_l=got_l, got_r=got_r):
            arrived(got_l, s_part.at[0])
            arrived(got_r, s_part.at[1])

        @pl.when(ok & has_l)
        def _(hr_=hr_, d=d):
            arrived(win.at[1, pl.ds(hr_, 128)], s_fan.at[d, 0])

        @pl.when(ok & has_r)
        def _(hr_=hr_, d=d):
            arrived(win.at[2, pl.ds(hr_, 128)], s_fan.at[d, 1])

        x = jnp.concatenate([win[blk, pl.ds(hr_, 128)] for blk in range(4)], 1)
        x = jnp.tanh(0.25 * x.astype(F32)).astype(BF16)
        lift[...] += mm(ta[A_FWD : A_FWD + 256, pl.ds(hr_, 128)], x)
    lift_b = lift[...].astype(BF16)
    s = mm(lift_b, tb[B_FT : B_FT + 512])
    spec[0] = s[:128, :128] - s[128:, 128:]
    spec[1] = s[:128, 128:] + s[128:, :128]

    dose = dose_ref[0]
    sre, sim = spec[0], spec[1]
    for k in range(KERNELS):
        kr, ki = kern[0, k, 0], kern[0, k, 1]
        bre = (kr * sre - ki * sim).astype(BF16)
        bim = (kr * sim + ki * sre).astype(BF16)
        blur = jnp.concatenate(
            [jnp.concatenate([bre, bim], 1), jnp.concatenate([-bim, bre], 1)], 0
        )
        proj[256 * k : 256 * k + 256] = mm(tb[B_INV : B_INV + 256], blur).astype(BF16)
    for k in range(KERNELS):
        fields[k] = mm(proj[256 * k : 256 * k + 256], ta[A_FIELD : A_FIELD + 256])
    total = jnp.zeros((TILE, TILE), F32)
    for k in range(KERNELS):
        fre, fim = fields[k, :, :256], fields[k, :, 256:]
        total = total + (fre * fre + fim * fim)
    inten[...] = total

    res = jax.nn.sigmoid(STEEPNESS * (dose * inten[...] - THRESHOLD))
    resist[...] = res
    cp_resist = local(resist, resist_hbm.at[0], out_sem.at[0])
    goal = target_i[...].astype(F32)
    sens2[...] = 2.0 * (2.0 * (res - goal) * STEEPNESS * dose * res * (1.0 - res))
    s2 = jnp.concatenate([sens2[...], sens2[...]], 1)
    for k in range(KERNELS):
        adj = (s2 * fields[k]).astype(BF16)
        proj[256 * k : 256 * k + 256] = mm(adj, tb[B_BACK : B_BACK + 512]).astype(BF16)
    acc_re = jnp.zeros((KF, KF), F32)
    acc_im = jnp.zeros((KF, KF), F32)
    for k in range(KERNELS):
        kr, ki = kern[0, k, 0], kern[0, k, 1]
        g = mm(tb[B_INVT : B_INVT + 256], proj[256 * k : 256 * k + 256])
        gre = g[:128, :128] + g[128:, 128:]
        gim = g[:128, 128:] - g[128:, :128]
        acc_re = acc_re + (kr * gre + ki * gim)
        acc_im = acc_im + (kr * gim - ki * gre)
    gacc[:, :128] = acc_re
    gacc[:, 128:] = acc_im

    cc = remote(16, gacc, gother, s_corner, partner)
    cc.start()
    started.append((c >= 0, (cc,)))
    arrived(gother, s_corner)
    hbuf[1] = (gacc[...] + gother[...]).astype(BF16)
    hl = remote(17, hbuf.at[1], hbuf.at[2], s_spec.at[1], left)
    hr = remote(18, hbuf.at[1], hbuf.at[0], s_spec.at[0], right)

    start(has_l, hl)
    start(has_r, hr)

    glift[0:128] = mm(hbuf[1], ta[A_FWD : A_FWD + 256])
    glift[128:256] = mm(hbuf[1], ta[A_TURN : A_TURN + 256])

    rows0 = pl.multiple_of(128 + 128 * c, 128)
    below = pl.multiple_of(256 + 128 * c, 128)
    above = pl.multiple_of(112 + 128 * c, 16)
    lane = lax.broadcasted_iota(jnp.int32, (EXT, 128), 1)

    def level_rows(blk):
        main = win[blk, pl.ds(rows0, 128)].astype(F32)
        after = win[blk, pl.ds(below, 16)].astype(F32)[0:8]
        before = win[blk, pl.ds(above, 16)].astype(F32)[8:16]
        return jnp.concatenate([main, after, before], 0)

    def ring(x, y):
        return jnp.where(lane < 64, x, y)

    level = jnp.concatenate([level_rows(1), level_rows(2), ring(level_rows(3), level_rows(0))], 1)
    trans = jnp.tanh(0.25 * level)
    final[:, 0:LANES] = level
    final[:, LANES : 2 * LANES] = 0.25 * (1.0 - trans * trans)

    @pl.when(has_l)
    def _():
        arrived(hbuf.at[0], s_spec.at[0])

    @pl.when(has_r)
    def _():
        arrived(hbuf.at[2], s_spec.at[1])

    for r, q in ((0, A_FWD), (128, A_TURN)):
        glift[r : r + 128, 0:256] += mm(hbuf[0], ta[q : q + 256, 256:512])
        glift[r : r + 128, 256:512] += mm(hbuf[2], ta[q : q + 256, 0:256])
    gl = glift[...].astype(BF16)

    gblk = [glift[:, 128 * i : 128 * i + 128] for i in range(4)]
    out_l = jnp.where(has_l, gblk[0], gblk[1]).astype(BF16)
    out_r = jnp.where(has_r, gblk[3], gblk[2]).astype(BF16)
    strip = mm(tb[pl.ds(pl.multiple_of(B_STRIP + EXT * c, 16), EXT)], jnp.concatenate([out_l, out_r], 1))
    pick_l = one_hot((16, 128), [(0, 0), (1, 1), (2, 0), (3, 1)])
    pick_r = one_hot((16, 128), [(0, 126), (1, 127), (2, 126), (3, 127)])
    picked = jnp.concatenate([mm_nt(pick_l, gl[:, 128:256]), mm_nt(pick_r, gl[:, 256:384])], 0)
    crossed = mm(picked.astype(BF16), tb[pl.ds(pl.multiple_of(B_CROSS + 256 * c, 16), 256)])
    row16 = lax.broadcasted_iota(jnp.int32, (16, 128), 0)
    for side in range(2):
        cols = slice(128 * side, 128 * side + 128)
        cr = crossed[16 * side : 16 * side + 16]
        edge = jnp.where(row16 < 2, cr[:, :128], cr[:, 128:])[0:8]
        part = strip[:, cols]
        near_rows = jnp.where(is0, part[8:16], part[0:8])
        msg_s[side, 0:16] = jnp.concatenate([edge, near_rows], 0).astype(BF16)
        msg_s[side, 16:EXT] = part[16:EXT].astype(BF16)
        tail_rows = jnp.where(is0, part[136:144], part[16:24])
        small_s[side] = jnp.concatenate([edge, tail_rows], 0).astype(BF16)

    ml = remote(19, msg_s.at[0], msg_r.at[1 - zl], s_msg.at[1 - zl], (ar, bl, c))
    mr = remote(20, msg_s.at[1], msg_r.at[zr], s_msg.at[zr], (ar, br, c))
    nl = remote(21, small_s.at[0], small_r.at[1 - zl], s_small.at[1 - zl], (ar, bl, other))
    nr = remote(22, small_s.at[1], small_r.at[zr], s_small.at[zr], (ar, br, other))

    @pl.when(hops)
    def _():
        pl.semaphore_wait(ready, 4)

    start(send_ok, ml, mr, nl, nr)

    ring_lane = lax.broadcasted_iota(jnp.int32, (256, 128), 1)
    gl_ring = jnp.where(ring_lane < 64, gblk[3], gblk[0]).astype(BF16)
    own_rows = tb[pl.ds(pl.multiple_of(B_OWN + EXT * c, 16), EXT)]
    grad = mm(own_rows, jnp.concatenate([gl[:, 128:384], gl_ring], 1))

    @pl.when(recv_ok)
    def _():
        arrived(msg_r.at[0], s_msg.at[0])
        arrived(msg_r.at[1], s_msg.at[1])

    @pl.when(small_ok)
    def _():
        arrived(small_r.at[0], s_small.at[0])
        arrived(small_r.at[1], s_small.at[1])

    eye = one_hot((128, 128), [])
    r128 = lax.broadcasted_iota(jnp.int32, (128, 128), 0)
    c128 = lax.broadcasted_iota(jnp.int32, (128, 128), 1)
    eye = jnp.where(r128 == c128, 1.0, 0.0).astype(BF16)
    sel_a = one_hot((32, 128), [(0, 126), (1, 127), (16, 0), (17, 1)])
    sel_b = one_hot((32, 128), [(2, 126), (3, 127), (18, 0), (19, 1)])
    edges = jnp.concatenate([msg_r[0, 0:16], msg_r[1, 0:16]], 0)
    edges_s = jnp.concatenate([small_r[0], small_r[1]], 0)
    turned = mm_nt(eye, edges).astype(BF16)
    turned_s = mm_nt(eye, edges_s).astype(BF16)
    col_main = mm(turned, sel_a)
    col_far = mm(turned, sel_b)
    col_small = mm(turned_s, sel_a)

    def add_part(blocks_main, blocks_ext, blocks_small):
        main = jnp.concatenate(blocks_main, 1)
        far = jnp.concatenate(blocks_ext, 1)
        near = jnp.concatenate(blocks_small, 1)
        after = jnp.where(is0, near[0:8], far[0:8])
        before = jnp.where(is0, far[8:16], near[8:16])
        return jnp.concatenate([main, after, before], 0)

    def twice(x):
        rows = x.astype(F32)[8:16]
        return jnp.concatenate([rows, rows], 0)

    col_far16 = jnp.concatenate([col_far[0:8], col_far[120:128]], 0)
    col_small16 = jnp.concatenate([col_small[0:8], col_small[120:128]], 0)
    received = add_part(
        [msg_r[0, 16:EXT].astype(F32), msg_r[1, 16:EXT].astype(F32), col_main],
        [twice(msg_r[0, 0:16]), twice(msg_r[1, 0:16]), col_far16],
        [twice(small_r[0]), twice(small_r[1]), col_small16],
    )
    speed = SPEED_GAIN * (grad + received) * final[:, LANES : 2 * LANES]

    row = lax.broadcasted_iota(jnp.int32, (EXT, LANES), 0)
    col = lax.broadcasted_iota(jnp.int32, (EXT, LANES), 1)
    i_off = jnp.where(row < 136, row, row - EXT) + 128 * c
    j_off = jnp.where(col < 320, col, col - LANES)
    i_all = a * TILE + i_off
    j_all = b * TILE + j_off
    inside = (i_all >= 0) & (i_all < n_ty * TILE) & (j_all >= 0) & (j_all < n_tx * TILE)

    level = final[:, 0:LANES]
    for _ in range(LS_STEPS):
        up = pltpu.roll(level, 1, 0)
        down = pltpu.roll(level, EXT - 1, 0)
        lf = pltpu.roll(level, 1, 1)
        rt = pltpu.roll(level, LANES - 1, 1)
        sy = 0.5 * (down - up)
        sx = 0.5 * (rt - lf)
        spread = up + down + lf + rt - 4.0 * level
        level = level - speed * jnp.sqrt(GRAD_FLOOR + sy * sy + sx * sx) + SMOOTHING * spread
        level = jnp.where(inside, level, 0.0)
    final[0:128, 0:256] = level[0:128, 0:256]

    mine = out_hbm.at[pl.ds(pl.multiple_of(128 * c, 128), 128)]
    result = final.at[pl.ds(0, 128), pl.ds(0, 256)]
    ff = remote(23, result, mine, s_final, partner)
    ff.start()
    started.append((c >= 0, (ff,)))
    cp_out = local(result, mine, out_sem.at[1])

    cp_resist.wait()
    cp_out.wait()
    settle()
    arrived(out_hbm.at[pl.ds(pl.multiple_of(128 * other, 128), 128)], s_final)


def make_body(n_ty, n_tx):
    def body(level_init, target, kernels, corner_doses):
        ta, tb = wide_tables()
        dma = pltpu.SemaphoreType.DMA
        anywhere = pl.BlockSpec(memory_space=pl.ANY)

        def whole(*args):
            return kernel(n_ty, n_tx, *args)

        return pl.pallas_call(
            whole,
            out_shape=(
                jax.ShapeDtypeStruct((1, TILE, TILE), F32),
                jax.ShapeDtypeStruct((TILE, TILE), F32),
            ),
            in_specs=[
                anywhere,
                anywhere,
                anywhere,
                pl.BlockSpec(memory_space=pltpu.SMEM),
                anywhere,
                anywhere,
            ],
            out_specs=(anywhere, anywhere),
            scratch_shapes=[
                pltpu.VMEM((TILE, TILE), jnp.int32),
                pltpu.VMEM((TILE, TILE), jnp.int32),
                pltpu.VMEM((1, KERNELS, 2, KF, KF), F32),
                pltpu.VMEM((A_ROWS, 512), BF16),
                pltpu.VMEM((B_ROWS, 256), BF16),
                pltpu.VMEM((4, WIN, 128), BF16),
                pltpu.VMEM((WIN, WIN), BF16),
                pltpu.VMEM((2, KF, KF), F32),
                pltpu.VMEM((KERNELS, TILE, 2 * TILE), F32),
                pltpu.VMEM((KERNELS * TILE, TILE), BF16),
                pltpu.VMEM((TILE, TILE), F32),
                pltpu.VMEM((TILE, TILE), F32),
                pltpu.VMEM((TILE, TILE), F32),
                pltpu.VMEM((KF, 2 * KF), F32),
                pltpu.VMEM((KF, 2 * KF), F32),
                pltpu.VMEM((3, KF, 2 * KF), BF16),
                pltpu.VMEM((2 * KF, WIN), F32),
                pltpu.VMEM((2 * KF, WIN), F32),
                pltpu.VMEM((2, EXT, 128), BF16),
                pltpu.VMEM((2, EXT, 128), BF16),
                pltpu.VMEM((2, 16, 128), BF16),
                pltpu.VMEM((2, 16, 128), BF16),
                pltpu.VMEM((EXT, 2 * LANES), F32),
                pltpu.VMEM((2, 128, 128), BF16),
                dma((5,)),
                dma((2,)),
                dma((28,)),
                dma((2,)),
                dma((2,)),
                dma((2, 2)),
                dma((2,)),
                dma,
                dma((2,)),
                dma((2,)),
                dma((2,)),
                dma,
                dma((2,)),
                pltpu.SemaphoreType.REGULAR,
                pltpu.SemaphoreType.REGULAR,
            ],
            compiler_params=pltpu.CompilerParams(
                collective_id=0,
                has_side_effects=True,
                vmem_limit_bytes=54600 * 1024,
            ),
            cost_estimate=pl.CostEstimate(
                flops=1_500_000_000, bytes_accessed=6_000_000, transcendentals=400_000
            ),
        )(level_init, target, kernels, corner_doses, jnp.asarray(ta), jnp.asarray(tb))

    return body


def solution(mesh):
    in_specs = (P("ty", "tx"), P("ty", "tx"), P("corner", None, None, None, None), P("corner"))
    out_specs = (P("corner", "ty", "tx"), P("ty", "tx"))
    return jax.shard_map(
        make_body(mesh.shape["ty"], mesh.shape["tx"]),
        mesh=mesh,
        in_specs=in_specs,
        out_specs=out_specs,
        check_vma=False,
    )
```

```python
import math

import jax
import jax.numpy as jnp
import ml_dtypes
import numpy as np
from jax import lax
from jax.experimental import pallas as pl
from jax.experimental.pallas import tpu as pltpu
from jax.sharding import PartitionSpec as P

TILE = 256
HALO = 128
KF = 128
WIN = 512
KERNELS = 5
LS_STEPS = 3

STEEPNESS = 4.0
THRESHOLD = 1.0
SPEED_GAIN = 4.0
SMOOTHING = 0.24
GRAD_FLOOR = 0.25

MESH = pl.DeviceIdType.MESH
F32 = jnp.float32
BF16 = jnp.bfloat16

EXT = 144
LANES = 384


def wide_tables():
    shifts = np.arange(KF, dtype=np.int32) - KF // 2
    places = np.arange(WIN, dtype=np.int32)
    phases = (shifts[:, None] * places[None, :]) % WIN
    angles = np.float32(2.0 * math.pi / WIN) * phases.astype(np.float32)
    scaled = np.float32(1.0 / math.sqrt(WIN))
    fc = np.cos(angles, dtype=np.float32) * scaled
    fs = -np.sin(angles, dtype=np.float32) * scaled
    inner = angles[:, HALO : HALO + TILE].T
    ic = np.cos(inner, dtype=np.float32) * scaled
    isn = np.sin(inner, dtype=np.float32) * scaled
    fwd = np.concatenate([fc, fs], 0)
    turn = np.concatenate([-fs, fc], 0)
    to_field = np.concatenate(
        [np.concatenate([ic.T, isn.T], 1), np.concatenate([-isn.T, ic.T], 1)], 0
    )
    inv = np.concatenate([ic, isn], 1)
    ft = fwd.T
    lo, hi = HALO, HALO + 128
    own = [
        np.concatenate([ft[lo:hi], ft[hi : hi + 8], ft[lo - 8 : lo]], 0),
        np.concatenate([ft[hi : hi + 128], ft[hi + 128 : hi + 136], ft[hi - 8 : hi]], 0),
    ]
    strip = [ft[368:512], np.concatenate([ft[128:144], ft[0:128]], 0)]
    cross = [
        np.concatenate([fwd[:, 384:512], fwd[:, 256:384]], 1),
        fwd[:, 0:256],
    ]
    a = np.concatenate([fwd, turn, to_field], 0)
    b = np.concatenate([ft, inv, to_field.T, inv.T] + own + strip + cross, 0)
    return a.astype(ml_dtypes.bfloat16), b.astype(ml_dtypes.bfloat16)


A_FWD, A_TURN, A_FIELD, A_ROWS = 0, 256, 512, 768
B_FT, B_INV, B_BACK, B_INVT, B_OWN = 0, 512, 768, 1280, 1536
B_STRIP = B_OWN + 2 * EXT
B_CROSS = B_STRIP + 2 * EXT
B_ROWS = B_CROSS + 512


def mm(x, y):
    return jnp.dot(x, y, preferred_element_type=F32)


def mm_nt(x, y):
    return lax.dot_general(x, y, (((1,), (1,)), ((), ())), preferred_element_type=F32)


def one_hot(shape, pairs):
    rows = lax.broadcasted_iota(jnp.int32, shape, 0)
    cols = lax.broadcasted_iota(jnp.int32, shape, 1)
    hit = jnp.zeros(shape, F32)
    for r, c in pairs:
        hit = jnp.where((rows == r) & (cols == c), 1.0, hit)
    return hit.astype(BF16)


def kernel(
    n_ty,
    n_tx,
    level_hbm,
    target_hbm,
    kern_hbm,
    dose_ref,
    a_hbm,
    b_hbm,
    resist_hbm,
    out_hbm,
    level_i,
    target_i,
    kern,
    ta,
    tb,
    win,
    trw,
    spec,
    fields,
    proj,
    inten,
    sens2,
    resist,
    gacc,
    gother,
    hbuf,
    lift,
    glift,
    msg_s,
    msg_r,
    small_s,
    small_r,
    final,
    done,
    held,
    in_sem,
    out_sem,
    send,
    s_side,
    s_far,
    s_fan,
    s_part,
    s_corner,
    s_spec,
    s_msg,
    s_small,
    s_final,
    s_held,
    ready,
    ready_relay,
):
    a, b, c = lax.axis_index("ty"), lax.axis_index("tx"), lax.axis_index("corner")
    has_l, has_r = b > 0, b < n_tx - 1
    up_ok, dn_ok = a > 0, a < n_ty - 1
    is0 = c == 0
    send_ok = jnp.where(is0, dn_ok.astype(jnp.int32), up_ok.astype(jnp.int32)) > 0
    recv_ok = jnp.where(is0, up_ok.astype(jnp.int32), dn_ok.astype(jnp.int32)) > 0
    ar = a + 1 - 2 * c
    bl, br = jnp.maximum(b - 1, 0), jnp.minimum(b + 1, n_tx - 1)
    zl, zr = jnp.where(has_l, 0, 1), jnp.where(has_r, 0, 1)
    other = 1 - c

    early_dn, early_up = (a % 8 == 3) & dn_ok, (a % 8 == 0) & up_ok
    late_up, late_dn = (a % 8 == 4) & up_ok, (a % 8 == 7) & dn_ok
    early, late = early_dn | early_up, late_up | late_dn
    far_row = jnp.where(early_dn | late_dn, a + 1, a - 1)
    far_core = jnp.where(early_dn | late_up, 0, 1)
    hops = early & (c == far_core)
    meets = late & (c == far_core)
    half = n_tx // 2
    bp = (b + half) % n_tx
    bpl, bpr = jnp.maximum(bp - 1, 0), jnp.minimum(bp + 1, n_tx - 1)
    zpl, zpr = jnp.where(bp > 0, 0, 1), jnp.where(bp < n_tx - 1, 0, 1)
    straight = send_ok & jnp.logical_not(hops)
    left, right, partner = (a, b - 1, c), (a, b + 1, c), (a, b, other)

    def local(src, dst, sem):
        cp = pltpu.make_async_copy(src, dst, sem)
        cp.start()
        return cp

    def remote(i, src, dst, rsem, dev):
        return pltpu.make_async_remote_copy(
            src_ref=src,
            dst_ref=dst,
            send_sem=send.at[i],
            recv_sem=rsem,
            device_id=dev,
            device_id_type=MESH,
        )

    def arrived(dst, rsem):
        pltpu.make_async_remote_copy(
            src_ref=dst,
            dst_ref=dst,
            send_sem=send.at[0],
            recv_sem=rsem,
            device_id=partner,
            device_id_type=MESH,
        ).wait_recv()

    started = []

    def start(cond, *copies):
        started.append((cond, copies))

        @pl.when(cond)
        def _():
            for d in copies:
                d.start()

    def settle():
        for cond, copies in started:

            @pl.when(cond)
            def _(copies=copies):
                for d in copies:
                    d.wait_send()

    barrier = pltpu.get_barrier_semaphore()

    def hello(dev):
        pl.semaphore_signal(barrier, inc=1, device_id=dev, device_id_type=MESH)

    @pl.when(hops)
    def _():
        hello((a, bp, c))
        hello((far_row, bl, c))
        hello((far_row, br, c))
        hello((far_row, bpl, c))
        hello((far_row, bpr, c))

    @pl.when(up_ok & jnp.logical_not(late_up))
    def _():
        hello((a - 1, bl, 0))
        hello((a - 1, br, 0))

    @pl.when(dn_ok & jnp.logical_not(late_dn))
    def _():
        hello((a + 1, bl, 1))
        hello((a + 1, br, 1))

    hello(partner)

    @pl.when(has_l)
    def _():
        hello((a, b - 1, 0))
        hello((a, b - 1, 1))

    @pl.when(has_r)
    def _():
        hello((a, b + 1, 0))
        hello((a, b + 1, 1))

    cp_level = local(level_hbm, level_i, in_sem.at[0])
    cp_a = local(a_hbm, ta, in_sem.at[1])
    cp_kern = local(kern_hbm, kern, in_sem.at[2])
    cp_b = local(b_hbm, tb, in_sem.at[3])
    cp_target = local(target_hbm, target_i, in_sem.at[4])

    cp_level.wait()
    level0 = level_i[...].astype(F32) * 0.125
    low = level0.astype(BF16)
    win[1, 128:384] = low[:, :128]
    win[2, 128:384] = low[:, 128:]

    wanted = (
        1
        + 2 * has_l.astype(jnp.int32)
        + 2 * has_r.astype(jnp.int32)
        + 4 * straight.astype(jnp.int32)
        + hops.astype(jnp.int32)
        + 4 * meets.astype(jnp.int32)
    )
    pl.semaphore_wait(barrier, wanted)

    @pl.when(meets)
    def _():
        for to in (bl, br):
            pl.semaphore_signal(
                ready_relay,
                inc=1,
                device_id=(far_row, (to + half) % n_tx, far_core),
                device_id_type=MESH,
            )

    @pl.when(late)
    def _():
        for to in (bl, br):
            pl.semaphore_signal(ready, inc=1, device_id=(far_row, to, far_core), device_id_type=MESH)

    srow = pl.multiple_of(256 - 128 * c, 128)
    hrow = pl.multiple_of(384 * c, 128)
    fl = remote(0, win.at[1, pl.ds(srow, 128)], win.at[jnp.where(has_l, 3, 1), pl.ds(hrow, 128)], s_far.at[1 - zl], (ar, bl, c))
    fr = remote(1, win.at[2, pl.ds(srow, 128)], win.at[jnp.where(has_r, 0, 2), pl.ds(hrow, 128)], s_far.at[zr], (ar, br, c))
    sl = remote(2, win.at[1, pl.ds(128, 256)], win.at[3, pl.ds(128, 256)], s_side.at[1], left)
    sr = remote(3, win.at[2, pl.ds(128, 256)], win.at[0, pl.ds(128, 256)], s_side.at[0], right)

    kl = remote(24, win.at[1, pl.ds(srow, 128)], held.at[0], s_held.at[0], (a, bp, c))
    kr_ = remote(25, win.at[2, pl.ds(srow, 128)], held.at[1], s_held.at[1], (a, bp, c))
    ol = remote(26, held.at[0], win.at[jnp.where(bp > 0, 3, 1), pl.ds(hrow, 128)], s_far.at[1 - zpl], (far_row, bpl, c))
    orr = remote(27, held.at[1], win.at[jnp.where(bp < n_tx - 1, 0, 2), pl.ds(hrow, 128)], s_far.at[zpr], (far_row, bpr, c))

    start(hops, kl, kr_)
    start(straight, fl, fr)
    start(has_l, sl)
    start(has_r, sr)

    @pl.when(jnp.logical_not(has_l))
    def _():
        win[0] = jnp.zeros((WIN, 128), BF16)
        hbuf[0] = jnp.zeros((KF, 256), BF16)

    @pl.when(jnp.logical_not(has_r))
    def _():
        win[3] = jnp.zeros((WIN, 128), BF16)
        hbuf[2] = jnp.zeros((KF, 256), BF16)

    for q, ok in ((0, up_ok), (384, dn_ok)):
        @pl.when(jnp.logical_not(ok))
        def _(q=q):
            for blk in range(4):
                win[blk, q : q + 128] = jnp.zeros((128, 128), BF16)

    @pl.when(jnp.logical_not(recv_ok))
    def _():
        msg_r[...] = jnp.zeros_like(msg_r)

    small_ok = jnp.where(is0, dn_ok.astype(jnp.int32), up_ok.astype(jnp.int32)) > 0

    @pl.when(jnp.logical_not(small_ok))
    def _():
        small_r[...] = jnp.zeros_like(small_r)

    def to_trans(blk, r0, rows):
        x = win[blk, r0 : r0 + rows].astype(F32)
        trw[r0 : r0 + rows, blk * 128 : blk * 128 + 128] = jnp.tanh(0.25 * x).astype(BF16)

    to_trans(1, 128, 256)
    to_trans(2, 128, 256)

    @pl.when(has_l)
    def _():
        arrived(win.at[0, pl.ds(128, 256)], s_side.at[0])

    to_trans(0, 128, 256)

    @pl.when(has_r)
    def _():
        arrived(win.at[3, pl.ds(128, 256)], s_side.at[1])

    to_trans(3, 128, 256)
    cp_a.wait()
    cp_b.wait()
    cp_kern.wait()
    cp_target.wait()
    lift[...] = mm(ta[A_FWD : A_FWD + 256, 128:384], trw[128:384, :])

    @pl.when(hops)
    def _():
        pl.semaphore_wait(ready_relay, 2)
        arrived(held.at[0], s_held.at[0])
        ol.start()
        arrived(held.at[1], s_held.at[1])
        orr.start()

    started.append((hops, (ol, orr)))

    blk_l, blk_r = jnp.where(has_l, 0, 1), jnp.where(has_r, 3, 2)
    first = jnp.where(late_up | early_up, 1, jnp.where(late_dn | early_dn, 0, c))
    for step in range(2):
        d = first if step == 0 else 1 - first
        ok = jnp.where(d == 0, up_ok.astype(jnp.int32), dn_ok.astype(jnp.int32)) > 0
        mine, theirs = ok & (d == c), ok & (d != c)
        hr_ = pl.multiple_of(384 * d, 128)
        got_l, got_r = win.at[blk_l, pl.ds(hr_, 128)], win.at[blk_r, pl.ds(hr_, 128)]
        n0 = 4 + 6 * step
        part_l = remote(n0, got_l, got_l, s_part.at[0], partner)
        part_r = remote(n0 + 1, got_r, got_r, s_part.at[1], partner)
        fan_l = [
            remote(n0 + 2 + e, got_l, win.at[2, pl.ds(hr_, 128)], s_fan.at[d, 1], (a, b - 1, e))
            for e in (0, 1)
        ]
        fan_r = [
            remote(n0 + 4 + e, got_r, win.at[1, pl.ds(hr_, 128)], s_fan.at[d, 0], (a, b + 1, e))
            for e in (0, 1)
        ]

        @pl.when(mine)
        def _(got=got_l):
            arrived(got, s_far.at[0])

        start(mine & has_l, *fan_l)
        start(mine, part_l)

        @pl.when(mine)
        def _(got=got_r):
            arrived(got, s_far.at[1])

        start(mine & has_r, *fan_r)
        start(mine, part_r)

        @pl.when(theirs)
        def _(got_l=got_l, got_r=got_r):
            arrived(got_l, s_part.at[0])
            arrived(got_r, s_part.at[1])

        @pl.when(ok & has_l)
        def _(hr_=hr_, d=d):
            arrived(win.at[1, pl.ds(hr_, 128)], s_fan.at[d, 0])

        @pl.when(ok & has_r)
        def _(hr_=hr_, d=d):
            arrived(win.at[2, pl.ds(hr_, 128)], s_fan.at[d, 1])

        x = jnp.concatenate([win[blk, pl.ds(hr_, 128)] for blk in range(4)], 1)
        x = jnp.tanh(0.25 * x.astype(F32)).astype(BF16)
        lift[...] += mm(ta[A_FWD : A_FWD + 256, pl.ds(hr_, 128)], x)
    lift_b = lift[...].astype(BF16)
    s = mm(lift_b, tb[B_FT : B_FT + 512])
    spec[0] = s[:128, :128] - s[128:, 128:]
    spec[1] = s[:128, 128:] + s[128:, :128]

    dose = dose_ref[0]
    sre, sim = spec[0], spec[1]
    for k in range(KERNELS):
        kr, ki = kern[0, k, 0], kern[0, k, 1]
        bre = (kr * sre - ki * sim).astype(BF16)
        bim = (kr * sim + ki * sre).astype(BF16)
        blur = jnp.concatenate(
            [jnp.concatenate([bre, bim], 1), jnp.concatenate([-bim, bre], 1)], 0
        )
        proj[256 * k : 256 * k + 256] = mm(tb[B_INV : B_INV + 256], blur).astype(BF16)
    for k in range(KERNELS):
        fields[k] = mm(proj[256 * k : 256 * k + 256], ta[A_FIELD : A_FIELD + 256])
    total = jnp.zeros((TILE, TILE), F32)
    for k in range(KERNELS):
        fre, fim = fields[k, :, :256], fields[k, :, 256:]
        total = total + (fre * fre + fim * fim)
    inten[...] = total

    res = jax.nn.sigmoid(STEEPNESS * (dose * inten[...] - THRESHOLD))
    resist[...] = res
    cp_resist = local(resist, resist_hbm.at[0], out_sem.at[0])
    goal = target_i[...].astype(F32)
    sens2[...] = 2.0 * (2.0 * (res - goal) * STEEPNESS * dose * res * (1.0 - res))
    s2 = jnp.concatenate([sens2[...], sens2[...]], 1)
    for k in range(KERNELS):
        adj = (s2 * fields[k]).astype(BF16)
        proj[256 * k : 256 * k + 256] = mm(adj, tb[B_BACK : B_BACK + 512]).astype(BF16)
    acc_re = jnp.zeros((KF, KF), F32)
    acc_im = jnp.zeros((KF, KF), F32)
    for k in range(KERNELS):
        kr, ki = kern[0, k, 0], kern[0, k, 1]
        g = mm(tb[B_INVT : B_INVT + 256], proj[256 * k : 256 * k + 256])
        gre = g[:128, :128] + g[128:, 128:]
        gim = g[:128, 128:] - g[128:, :128]
        acc_re = acc_re + (kr * gre + ki * gim)
        acc_im = acc_im + (kr * gim - ki * gre)
    gacc[:, :128] = acc_re
    gacc[:, 128:] = acc_im

    cc = remote(16, gacc, gother, s_corner, partner)
    cc.start()
    started.append((c >= 0, (cc,)))
    arrived(gother, s_corner)
    hbuf[1] = (gacc[...] + gother[...]).astype(BF16)
    hl = remote(17, hbuf.at[1], hbuf.at[2], s_spec.at[1], left)
    hr = remote(18, hbuf.at[1], hbuf.at[0], s_spec.at[0], right)

    start(has_l, hl)
    start(has_r, hr)

    glift[0:128] = mm(hbuf[1], ta[A_FWD : A_FWD + 256])
    glift[128:256] = mm(hbuf[1], ta[A_TURN : A_TURN + 256])

    rows0 = pl.multiple_of(128 + 128 * c, 128)
    below = pl.multiple_of(256 + 128 * c, 128)
    above = pl.multiple_of(112 + 128 * c, 16)
    lane = lax.broadcasted_iota(jnp.int32, (EXT, 128), 1)

    def level_rows(blk):
        main = win[blk, pl.ds(rows0, 128)].astype(F32)
        after = win[blk, pl.ds(below, 16)].astype(F32)[0:8]
        before = win[blk, pl.ds(above, 16)].astype(F32)[8:16]
        return jnp.concatenate([main, after, before], 0)

    def ring(x, y):
        return jnp.where(lane < 64, x, y)

    level = jnp.concatenate([level_rows(1), level_rows(2), ring(level_rows(3), level_rows(0))], 1)
    trans = jnp.tanh(0.25 * level)
    final[:, 0:LANES] = level
    final[:, LANES : 2 * LANES] = 0.25 * (1.0 - trans * trans)

    @pl.when(has_l)
    def _():
        arrived(hbuf.at[0], s_spec.at[0])

    @pl.when(has_r)
    def _():
        arrived(hbuf.at[2], s_spec.at[1])

    for r, q in ((0, A_FWD), (128, A_TURN)):
        glift[r : r + 128, 0:256] += mm(hbuf[0], ta[q : q + 256, 256:512])
        glift[r : r + 128, 256:512] += mm(hbuf[2], ta[q : q + 256, 0:256])
    gl = glift[...].astype(BF16)

    gblk = [glift[:, 128 * i : 128 * i + 128] for i in range(4)]
    out_l = jnp.where(has_l, gblk[0], gblk[1]).astype(BF16)
    out_r = jnp.where(has_r, gblk[3], gblk[2]).astype(BF16)
    strip = mm(tb[pl.ds(pl.multiple_of(B_STRIP + EXT * c, 16), EXT)], jnp.concatenate([out_l, out_r], 1))
    pick_l = one_hot((16, 128), [(0, 0), (1, 1), (2, 0), (3, 1)])
    pick_r = one_hot((16, 128), [(0, 126), (1, 127), (2, 126), (3, 127)])
    picked = jnp.concatenate([mm_nt(pick_l, gl[:, 128:256]), mm_nt(pick_r, gl[:, 256:384])], 0)
    crossed = mm(picked.astype(BF16), tb[pl.ds(pl.multiple_of(B_CROSS + 256 * c, 16), 256)])
    row16 = lax.broadcasted_iota(jnp.int32, (16, 128), 0)
    for side in range(2):
        cols = slice(128 * side, 128 * side + 128)
        cr = crossed[16 * side : 16 * side + 16]
        edge = jnp.where(row16 < 2, cr[:, :128], cr[:, 128:])[0:8]
        part = strip[:, cols]
        near_rows = jnp.where(is0, part[8:16], part[0:8])
        msg_s[side, 0:16] = jnp.concatenate([edge, near_rows], 0).astype(BF16)
        msg_s[side, 16:EXT] = part[16:EXT].astype(BF16)
        tail_rows = jnp.where(is0, part[136:144], part[16:24])
        small_s[side] = jnp.concatenate([edge, tail_rows], 0).astype(BF16)

    ml = remote(19, msg_s.at[0], msg_r.at[1 - zl], s_msg.at[1 - zl], (ar, bl, c))
    mr = remote(20, msg_s.at[1], msg_r.at[zr], s_msg.at[zr], (ar, br, c))
    nl = remote(21, small_s.at[0], small_r.at[1 - zl], s_small.at[1 - zl], (ar, bl, other))
    nr = remote(22, small_s.at[1], small_r.at[zr], s_small.at[zr], (ar, br, other))

    @pl.when(hops)
    def _():
        pl.semaphore_wait(ready, 4)

    start(send_ok, ml, mr, nl, nr)

    ring_lane = lax.broadcasted_iota(jnp.int32, (256, 128), 1)
    gl_ring = jnp.where(ring_lane < 64, gblk[3], gblk[0]).astype(BF16)
    own_rows = tb[pl.ds(pl.multiple_of(B_OWN + EXT * c, 16), EXT)]
    grad = mm(own_rows, jnp.concatenate([gl[:, 128:384], gl_ring], 1))

    @pl.when(recv_ok)
    def _():
        arrived(msg_r.at[0], s_msg.at[0])
        arrived(msg_r.at[1], s_msg.at[1])

    @pl.when(small_ok)
    def _():
        arrived(small_r.at[0], s_small.at[0])
        arrived(small_r.at[1], s_small.at[1])

    eye = one_hot((128, 128), [])
    r128 = lax.broadcasted_iota(jnp.int32, (128, 128), 0)
    c128 = lax.broadcasted_iota(jnp.int32, (128, 128), 1)
    eye = jnp.where(r128 == c128, 1.0, 0.0).astype(BF16)
    sel_a = one_hot((32, 128), [(0, 126), (1, 127), (16, 0), (17, 1)])
    sel_b = one_hot((32, 128), [(2, 126), (3, 127), (18, 0), (19, 1)])
    edges = jnp.concatenate([msg_r[0, 0:16], msg_r[1, 0:16]], 0)
    edges_s = jnp.concatenate([small_r[0], small_r[1]], 0)
    turned = mm_nt(eye, edges).astype(BF16)
    turned_s = mm_nt(eye, edges_s).astype(BF16)
    col_main = mm(turned, sel_a)
    col_far = mm(turned, sel_b)
    col_small = mm(turned_s, sel_a)

    def add_part(blocks_main, blocks_ext, blocks_small):
        main = jnp.concatenate(blocks_main, 1)
        far = jnp.concatenate(blocks_ext, 1)
        near = jnp.concatenate(blocks_small, 1)
        after = jnp.where(is0, near[0:8], far[0:8])
        before = jnp.where(is0, far[8:16], near[8:16])
        return jnp.concatenate([main, after, before], 0)

    def twice(x):
        rows = x.astype(F32)[8:16]
        return jnp.concatenate([rows, rows], 0)

    col_far16 = jnp.concatenate([col_far[0:8], col_far[120:128]], 0)
    col_small16 = jnp.concatenate([col_small[0:8], col_small[120:128]], 0)
    received = add_part(
        [msg_r[0, 16:EXT].astype(F32), msg_r[1, 16:EXT].astype(F32), col_main],
        [twice(msg_r[0, 0:16]), twice(msg_r[1, 0:16]), col_far16],
        [twice(small_r[0]), twice(small_r[1]), col_small16],
    )
    speed = SPEED_GAIN * (grad + received) * final[:, LANES : 2 * LANES]

    row = lax.broadcasted_iota(jnp.int32, (EXT, LANES), 0)
    col = lax.broadcasted_iota(jnp.int32, (EXT, LANES), 1)
    i_off = jnp.where(row < 136, row, row - EXT) + 128 * c
    j_off = jnp.where(col < 320, col, col - LANES)
    i_all = a * TILE + i_off
    j_all = b * TILE + j_off
    inside = (i_all >= 0) & (i_all < n_ty * TILE) & (j_all >= 0) & (j_all < n_tx * TILE)

    level = final[:, 0:LANES]
    for _ in range(LS_STEPS):
        up = pltpu.roll(level, 1, 0)
        down = pltpu.roll(level, EXT - 1, 0)
        lf = pltpu.roll(level, 1, 1)
        rt = pltpu.roll(level, LANES - 1, 1)
        sy = 0.5 * (down - up)
        sx = 0.5 * (rt - lf)
        spread = up + down + lf + rt - 4.0 * level
        level = level - speed * jnp.sqrt(GRAD_FLOOR + sy * sy + sx * sx) + SMOOTHING * spread
        level = jnp.where(inside, level, 0.0)
    done[...] = level[0:128, 0:256]

    mine = out_hbm.at[pl.ds(pl.multiple_of(128 * c, 128), 128)]
    result = done
    ff = remote(23, result, mine, s_final, partner)
    ff.start()
    started.append((c >= 0, (ff,)))
    cp_out = local(result, mine, out_sem.at[1])

    cp_resist.wait()
    cp_out.wait()
    settle()
    arrived(out_hbm.at[pl.ds(pl.multiple_of(128 * other, 128), 128)], s_final)


def make_body(n_ty, n_tx):
    def body(level_init, target, kernels, corner_doses):
        ta, tb = wide_tables()
        dma = pltpu.SemaphoreType.DMA
        anywhere = pl.BlockSpec(memory_space=pl.ANY)

        def whole(*args):
            return kernel(n_ty, n_tx, *args)

        return pl.pallas_call(
            whole,
            out_shape=(
                jax.ShapeDtypeStruct((1, TILE, TILE), F32),
                jax.ShapeDtypeStruct((TILE, TILE), F32),
            ),
            in_specs=[
                anywhere,
                anywhere,
                anywhere,
                pl.BlockSpec(memory_space=pltpu.SMEM),
                anywhere,
                anywhere,
            ],
            out_specs=(anywhere, anywhere),
            scratch_shapes=[
                pltpu.VMEM((TILE, TILE), jnp.int32),
                pltpu.VMEM((TILE, TILE), jnp.int32),
                pltpu.VMEM((1, KERNELS, 2, KF, KF), F32),
                pltpu.VMEM((A_ROWS, 512), BF16),
                pltpu.VMEM((B_ROWS, 256), BF16),
                pltpu.VMEM((4, WIN, 128), BF16),
                pltpu.VMEM((WIN, WIN), BF16),
                pltpu.VMEM((2, KF, KF), F32),
                pltpu.VMEM((KERNELS, TILE, 2 * TILE), F32),
                pltpu.VMEM((KERNELS * TILE, TILE), BF16),
                pltpu.VMEM((TILE, TILE), F32),
                pltpu.VMEM((TILE, TILE), F32),
                pltpu.VMEM((TILE, TILE), F32),
                pltpu.VMEM((KF, 2 * KF), F32),
                pltpu.VMEM((KF, 2 * KF), F32),
                pltpu.VMEM((3, KF, 2 * KF), BF16),
                pltpu.VMEM((2 * KF, WIN), F32),
                pltpu.VMEM((2 * KF, WIN), F32),
                pltpu.VMEM((2, EXT, 128), BF16),
                pltpu.VMEM((2, EXT, 128), BF16),
                pltpu.VMEM((2, 16, 128), BF16),
                pltpu.VMEM((2, 16, 128), BF16),
                pltpu.VMEM((EXT, 2 * LANES), F32),
                pltpu.VMEM((128, TILE), F32),
                pltpu.VMEM((2, 128, 128), BF16),
                dma((5,)),
                dma((2,)),
                dma((28,)),
                dma((2,)),
                dma((2,)),
                dma((2, 2)),
                dma((2,)),
                dma,
                dma((2,)),
                dma((2,)),
                dma((2,)),
                dma,
                dma((2,)),
                pltpu.SemaphoreType.REGULAR,
                pltpu.SemaphoreType.REGULAR,
            ],
            compiler_params=pltpu.CompilerParams(
                collective_id=0,
                has_side_effects=True,
                vmem_limit_bytes=54600 * 1024,
            ),
            cost_estimate=pl.CostEstimate(
                flops=1_500_000_000, bytes_accessed=6_000_000, transcendentals=400_000
            ),
        )(level_init, target, kernels, corner_doses, jnp.asarray(ta), jnp.asarray(tb))

    return body


def solution(mesh):
    in_specs = (P("ty", "tx"), P("ty", "tx"), P("corner", None, None, None, None), P("corner"))
    out_specs = (P("corner", "ty", "tx"), P("ty", "tx"))
    return jax.shard_map(
        make_body(mesh.shape["ty"], mesh.shape["tx"]),
        mesh=mesh,
        in_specs=in_specs,
        out_specs=out_specs,
        check_vma=False,
    )
```

```python
import math

import jax
import jax.numpy as jnp
import ml_dtypes
import numpy as np
from jax import lax
from jax.experimental import pallas as pl
from jax.experimental.pallas import tpu as pltpu
from jax.sharding import PartitionSpec as P

TILE = 256
HALO = 128
KF = 128
WIN = 512
KERNELS = 5
LS_STEPS = 3

STEEPNESS = 4.0
THRESHOLD = 1.0
SPEED_GAIN = 4.0
SMOOTHING = 0.24
GRAD_FLOOR = 0.25

MESH = pl.DeviceIdType.MESH
F32 = jnp.float32
BF16 = jnp.bfloat16

EXT = 144
LANES = 384


def wide_tables():
    shifts = np.arange(KF, dtype=np.int32) - KF // 2
    places = np.arange(WIN, dtype=np.int32)
    phases = (shifts[:, None] * places[None, :]) % WIN
    angles = np.float32(2.0 * math.pi / WIN) * phases.astype(np.float32)
    scaled = np.float32(1.0 / math.sqrt(WIN))
    fc = np.cos(angles, dtype=np.float32) * scaled
    fs = -np.sin(angles, dtype=np.float32) * scaled
    inner = angles[:, HALO : HALO + TILE].T
    ic = np.cos(inner, dtype=np.float32) * scaled
    isn = np.sin(inner, dtype=np.float32) * scaled
    fwd = np.concatenate([fc, fs], 0)
    turn = np.concatenate([-fs, fc], 0)
    to_field = np.concatenate(
        [np.concatenate([ic.T, isn.T], 1), np.concatenate([-isn.T, ic.T], 1)], 0
    )
    inv = np.concatenate([ic, isn], 1)
    ft = fwd.T
    lo, hi = HALO, HALO + 128
    own = [
        np.concatenate([ft[lo:hi], ft[hi : hi + 8], ft[lo - 8 : lo]], 0),
        np.concatenate([ft[hi : hi + 128], ft[hi + 128 : hi + 136], ft[hi - 8 : hi]], 0),
    ]
    strip = [ft[368:512], np.concatenate([ft[128:144], ft[0:128]], 0)]
    cross = [
        np.concatenate([fwd[:, 384:512], fwd[:, 256:384]], 1),
        fwd[:, 0:256],
    ]
    a = np.concatenate([fwd, turn, to_field], 0)
    b = np.concatenate([ft, inv, to_field.T, inv.T] + own + strip + cross, 0)
    return a.astype(ml_dtypes.bfloat16), b.astype(ml_dtypes.bfloat16)


A_FWD, A_TURN, A_FIELD, A_ROWS = 0, 256, 512, 768
B_FT, B_INV, B_BACK, B_INVT, B_OWN = 0, 512, 768, 1280, 1536
B_STRIP = B_OWN + 2 * EXT
B_CROSS = B_STRIP + 2 * EXT
B_ROWS = B_CROSS + 512


def mm(x, y):
    return jnp.dot(x, y, preferred_element_type=F32)


def mm_nt(x, y):
    return lax.dot_general(x, y, (((1,), (1,)), ((), ())), preferred_element_type=F32)


def one_hot(shape, pairs):
    rows = lax.broadcasted_iota(jnp.int32, shape, 0)
    cols = lax.broadcasted_iota(jnp.int32, shape, 1)
    hit = jnp.zeros(shape, F32)
    for r, c in pairs:
        hit = jnp.where((rows == r) & (cols == c), 1.0, hit)
    return hit.astype(BF16)


def kernel(
    n_ty,
    n_tx,
    level_hbm,
    target_hbm,
    kern_hbm,
    dose_ref,
    a_hbm,
    b_hbm,
    resist_hbm,
    out_hbm,
    level_i,
    target_i,
    kern,
    ta,
    tb,
    win,
    trw,
    spec,
    fields,
    proj,
    inten,
    sens2,
    resist,
    gacc,
    gother,
    hbuf,
    lift,
    glift,
    msg_s,
    msg_r,
    small_s,
    small_r,
    final,
    held,
    in_sem,
    out_sem,
    send,
    s_side,
    s_far,
    s_fan,
    s_part,
    s_corner,
    s_spec,
    s_msg,
    s_small,
    s_final,
    s_held,
    ready,
    ready_relay,
):
    a, b, c = lax.axis_index("ty"), lax.axis_index("tx"), lax.axis_index("corner")
    has_l, has_r = b > 0, b < n_tx - 1
    up_ok, dn_ok = a > 0, a < n_ty - 1
    is0 = c == 0
    send_ok = jnp.where(is0, dn_ok.astype(jnp.int32), up_ok.astype(jnp.int32)) > 0
    recv_ok = jnp.where(is0, up_ok.astype(jnp.int32), dn_ok.astype(jnp.int32)) > 0
    ar = a + 1 - 2 * c
    bl, br = jnp.maximum(b - 1, 0), jnp.minimum(b + 1, n_tx - 1)
    zl, zr = jnp.where(has_l, 0, 1), jnp.where(has_r, 0, 1)
    other = 1 - c

    early_dn, early_up = (a % 8 == 3) & dn_ok, (a % 8 == 0) & up_ok
    late_up, late_dn = (a % 8 == 4) & up_ok, (a % 8 == 7) & dn_ok
    early, late = early_dn | early_up, late_up | late_dn
    far_row = jnp.where(early_dn | late_dn, a + 1, a - 1)
    far_core = jnp.where(early_dn | late_up, 0, 1)
    hops = early & (c == far_core)
    meets = late & (c == far_core)
    half = n_tx // 2
    bp = (b + half) % n_tx
    bpl, bpr = jnp.maximum(bp - 1, 0), jnp.minimum(bp + 1, n_tx - 1)
    zpl, zpr = jnp.where(bp > 0, 0, 1), jnp.where(bp < n_tx - 1, 0, 1)
    straight = send_ok & jnp.logical_not(hops)
    left, right, partner = (a, b - 1, c), (a, b + 1, c), (a, b, other)

    def local(src, dst, sem):
        cp = pltpu.make_async_copy(src, dst, sem)
        cp.start()
        return cp

    def remote(i, src, dst, rsem, dev):
        return pltpu.make_async_remote_copy(
            src_ref=src,
            dst_ref=dst,
            send_sem=send.at[i],
            recv_sem=rsem,
            device_id=dev,
            device_id_type=MESH,
        )

    def arrived(dst, rsem):
        pltpu.make_async_remote_copy(
            src_ref=dst,
            dst_ref=dst,
            send_sem=send.at[0],
            recv_sem=rsem,
            device_id=partner,
            device_id_type=MESH,
        ).wait_recv()

    started = []

    def start(cond, *copies):
        started.append((cond, copies))

        @pl.when(cond)
        def _():
            for d in copies:
                d.start()

    def settle():
        for cond, copies in started:

            @pl.when(cond)
            def _(copies=copies):
                for d in copies:
                    d.wait_send()

    cp_level = local(level_hbm, level_i, in_sem.at[0])
    cp_a = local(a_hbm, ta, in_sem.at[1])
    cp_kern = local(kern_hbm, kern, in_sem.at[2])
    cp_b = local(b_hbm, tb, in_sem.at[3])
    cp_target = local(target_hbm, target_i, in_sem.at[4])

    barrier = pltpu.get_barrier_semaphore()

    def hello(dev):
        pl.semaphore_signal(barrier, inc=1, device_id=dev, device_id_type=MESH)

    @pl.when(up_ok & jnp.logical_not(late_up))
    def _():
        hello((a - 1, bl, 0))
        hello((a - 1, br, 0))

    @pl.when(dn_ok & jnp.logical_not(late_dn))
    def _():
        hello((a + 1, bl, 1))
        hello((a + 1, br, 1))

    @pl.when(hops)
    def _():
        hello((a, bp, c))
        hello((far_row, bl, c))
        hello((far_row, br, c))
        hello((far_row, bpl, c))
        hello((far_row, bpr, c))

    hello(partner)

    @pl.when(has_l)
    def _():
        hello((a, b - 1, 0))
        hello((a, b - 1, 1))

    @pl.when(has_r)
    def _():
        hello((a, b + 1, 0))
        hello((a, b + 1, 1))

    cp_level.wait()
    level0 = level_i[...].astype(F32) * 0.125
    low = level0.astype(BF16)
    win[1, 128:384] = low[:, :128]
    win[2, 128:384] = low[:, 128:]

    wanted = (
        1
        + 2 * has_l.astype(jnp.int32)
        + 2 * has_r.astype(jnp.int32)
        + 4 * straight.astype(jnp.int32)
        + hops.astype(jnp.int32)
        + 4 * meets.astype(jnp.int32)
    )
    pl.semaphore_wait(barrier, wanted)

    @pl.when(late)
    def _():
        for to in (bl, br):
            pl.semaphore_signal(ready, inc=1, device_id=(far_row, to, far_core), device_id_type=MESH)

    @pl.when(meets)
    def _():
        for to in (bl, br):
            pl.semaphore_signal(
                ready_relay,
                inc=1,
                device_id=(far_row, (to + half) % n_tx, far_core),
                device_id_type=MESH,
            )

    srow = pl.multiple_of(256 - 128 * c, 128)
    hrow = pl.multiple_of(384 * c, 128)
    fl = remote(0, win.at[1, pl.ds(srow, 128)], win.at[jnp.where(has_l, 3, 1), pl.ds(hrow, 128)], s_far.at[1 - zl], (ar, bl, c))
    fr = remote(1, win.at[2, pl.ds(srow, 128)], win.at[jnp.where(has_r, 0, 2), pl.ds(hrow, 128)], s_far.at[zr], (ar, br, c))
    sl = remote(2, win.at[1, pl.ds(128, 256)], win.at[3, pl.ds(128, 256)], s_side.at[1], left)
    sr = remote(3, win.at[2, pl.ds(128, 256)], win.at[0, pl.ds(128, 256)], s_side.at[0], right)

    kl = remote(24, win.at[1, pl.ds(srow, 128)], held.at[0], s_held.at[0], (a, bp, c))
    kr_ = remote(25, win.at[2, pl.ds(srow, 128)], held.at[1], s_held.at[1], (a, bp, c))
    ol = remote(26, held.at[0], win.at[jnp.where(bp > 0, 3, 1), pl.ds(hrow, 128)], s_far.at[1 - zpl], (far_row, bpl, c))
    orr = remote(27, held.at[1], win.at[jnp.where(bp < n_tx - 1, 0, 2), pl.ds(hrow, 128)], s_far.at[zpr], (far_row, bpr, c))

    start(hops, kl, kr_)
    start(straight, fl, fr)
    start(has_l, sl)
    start(has_r, sr)

    @pl.when(jnp.logical_not(has_l))
    def _():
        win[0] = jnp.zeros((WIN, 128), BF16)
        hbuf[0] = jnp.zeros((KF, 256), BF16)

    @pl.when(jnp.logical_not(has_r))
    def _():
        win[3] = jnp.zeros((WIN, 128), BF16)
        hbuf[2] = jnp.zeros((KF, 256), BF16)

    for q, ok in ((0, up_ok), (384, dn_ok)):
        @pl.when(jnp.logical_not(ok))
        def _(q=q):
            for blk in range(4):
                win[blk, q : q + 128] = jnp.zeros((128, 128), BF16)

    @pl.when(jnp.logical_not(recv_ok))
    def _():
        msg_r[...] = jnp.zeros_like(msg_r)

    small_ok = jnp.where(is0, dn_ok.astype(jnp.int32), up_ok.astype(jnp.int32)) > 0

    @pl.when(jnp.logical_not(small_ok))
    def _():
        small_r[...] = jnp.zeros_like(small_r)

    def to_trans(blk, r0, rows):
        x = win[blk, r0 : r0 + rows].astype(F32)
        trw[r0 : r0 + rows, blk * 128 : blk * 128 + 128] = jnp.tanh(0.25 * x).astype(BF16)

    to_trans(1, 128, 256)
    to_trans(2, 128, 256)

    @pl.when(has_l)
    def _():
        arrived(win.at[0, pl.ds(128, 256)], s_side.at[0])

    to_trans(0, 128, 256)

    @pl.when(has_r)
    def _():
        arrived(win.at[3, pl.ds(128, 256)], s_side.at[1])

    to_trans(3, 128, 256)
    cp_a.wait()
    cp_b.wait()
    cp_kern.wait()
    cp_target.wait()
    lift[...] = mm(ta[A_FWD : A_FWD + 256, 128:384], trw[128:384, :])

    @pl.when(hops)
    def _():
        pl.semaphore_wait(ready_relay, 2)
        arrived(held.at[0], s_held.at[0])
        ol.start()
        arrived(held.at[1], s_held.at[1])
        orr.start()

    started.append((hops, (ol, orr)))

    blk_l, blk_r = jnp.where(has_l, 0, 1), jnp.where(has_r, 3, 2)
    first = jnp.where(late_up | early_up, 1, jnp.where(late_dn | early_dn, 0, c))
    for step in range(2):
        d = first if step == 0 else 1 - first
        ok = jnp.where(d == 0, up_ok.astype(jnp.int32), dn_ok.astype(jnp.int32)) > 0
        mine, theirs = ok & (d == c), ok & (d != c)
        hr_ = pl.multiple_of(384 * d, 128)
        got_l, got_r = win.at[blk_l, pl.ds(hr_, 128)], win.at[blk_r, pl.ds(hr_, 128)]
        n0 = 4 + 6 * step
        part_l = remote(n0, got_l, got_l, s_part.at[0], partner)
        part_r = remote(n0 + 1, got_r, got_r, s_part.at[1], partner)
        fan_l = [
            remote(n0 + 2 + e, got_l, win.at[2, pl.ds(hr_, 128)], s_fan.at[d, 1], (a, b - 1, e))
            for e in (0, 1)
        ]
        fan_r = [
            remote(n0 + 4 + e, got_r, win.at[1, pl.ds(hr_, 128)], s_fan.at[d, 0], (a, b + 1, e))
            for e in (0, 1)
        ]

        @pl.when(mine)
        def _(got=got_l):
            arrived(got, s_far.at[0])

        start(mine & has_l, *fan_l)
        start(mine, part_l)

        @pl.when(mine)
        def _(got=got_r):
            arrived(got, s_far.at[1])

        start(mine & has_r, *fan_r)
        start(mine, part_r)

        @pl.when(theirs)
        def _(got_l=got_l, got_r=got_r):
            arrived(got_l, s_part.at[0])
            arrived(got_r, s_part.at[1])

        @pl.when(ok & has_l)
        def _(hr_=hr_, d=d):
            arrived(win.at[1, pl.ds(hr_, 128)], s_fan.at[d, 0])

        @pl.when(ok & has_r)
        def _(hr_=hr_, d=d):
            arrived(win.at[2, pl.ds(hr_, 128)], s_fan.at[d, 1])

        x = jnp.concatenate([win[blk, pl.ds(hr_, 128)] for blk in range(4)], 1)
        x = jnp.tanh(0.25 * x.astype(F32)).astype(BF16)
        lift[...] += mm(ta[A_FWD : A_FWD + 256, pl.ds(hr_, 128)], x)
    lift_b = lift[...].astype(BF16)
    s = mm(lift_b, tb[B_FT : B_FT + 512])
    spec[0] = s[:128, :128] - s[128:, 128:]
    spec[1] = s[:128, 128:] + s[128:, :128]

    dose = dose_ref[0]
    sre, sim = spec[0], spec[1]
    for k in range(KERNELS):
        kr, ki = kern[0, k, 0], kern[0, k, 1]
        bre = (kr * sre - ki * sim).astype(BF16)
        bim = (kr * sim + ki * sre).astype(BF16)
        blur = jnp.concatenate(
            [jnp.concatenate([bre, bim], 1), jnp.concatenate([-bim, bre], 1)], 0
        )
        proj[256 * k : 256 * k + 256] = mm(tb[B_INV : B_INV + 256], blur).astype(BF16)
    for k in range(KERNELS):
        fields[k] = mm(proj[256 * k : 256 * k + 256], ta[A_FIELD : A_FIELD + 256])
    total = jnp.zeros((TILE, TILE), F32)
    for k in range(KERNELS):
        fre, fim = fields[k, :, :256], fields[k, :, 256:]
        total = total + (fre * fre + fim * fim)
    inten[...] = total

    res = jax.nn.sigmoid(STEEPNESS * (dose * inten[...] - THRESHOLD))
    resist[...] = res
    cp_resist = local(resist, resist_hbm.at[0], out_sem.at[0])
    goal = target_i[...].astype(F32)
    sens2[...] = 2.0 * (2.0 * (res - goal) * STEEPNESS * dose * res * (1.0 - res))
    s2 = jnp.concatenate([sens2[...], sens2[...]], 1)
    for k in range(KERNELS):
        adj = (s2 * fields[k]).astype(BF16)
        proj[256 * k : 256 * k + 256] = mm(adj, tb[B_BACK : B_BACK + 512]).astype(BF16)
    acc_re = jnp.zeros((KF, KF), F32)
    acc_im = jnp.zeros((KF, KF), F32)
    for k in range(KERNELS):
        kr, ki = kern[0, k, 0], kern[0, k, 1]
        g = mm(tb[B_INVT : B_INVT + 256], proj[256 * k : 256 * k + 256])
        gre = g[:128, :128] + g[128:, 128:]
        gim = g[:128, 128:] - g[128:, :128]
        acc_re = acc_re + (kr * gre + ki * gim)
        acc_im = acc_im + (kr * gim - ki * gre)
    gacc[:, :128] = acc_re
    gacc[:, 128:] = acc_im

    cc = remote(16, gacc, gother, s_corner, partner)
    cc.start()
    started.append((c >= 0, (cc,)))
    arrived(gother, s_corner)
    hbuf[1] = (gacc[...] + gother[...]).astype(BF16)
    hl = remote(17, hbuf.at[1], hbuf.at[2], s_spec.at[1], left)
    hr = remote(18, hbuf.at[1], hbuf.at[0], s_spec.at[0], right)

    start(has_l, hl)
    start(has_r, hr)

    glift[0:128] = mm(hbuf[1], ta[A_FWD : A_FWD + 256])
    glift[128:256] = mm(hbuf[1], ta[A_TURN : A_TURN + 256])

    rows0 = pl.multiple_of(128 + 128 * c, 128)
    below = pl.multiple_of(256 + 128 * c, 128)
    above = pl.multiple_of(112 + 128 * c, 16)
    lane = lax.broadcasted_iota(jnp.int32, (EXT, 128), 1)

    def level_rows(blk):
        main = win[blk, pl.ds(rows0, 128)].astype(F32)
        after = win[blk, pl.ds(below, 16)].astype(F32)[0:8]
        before = win[blk, pl.ds(above, 16)].astype(F32)[8:16]
        return jnp.concatenate([main, after, before], 0)

    def ring(x, y):
        return jnp.where(lane < 64, x, y)

    level = jnp.concatenate([level_rows(1), level_rows(2), ring(level_rows(3), level_rows(0))], 1)
    trans = jnp.tanh(0.25 * level)
    final[:, 0:LANES] = level
    final[:, LANES : 2 * LANES] = 0.25 * (1.0 - trans * trans)

    @pl.when(has_l)
    def _():
        arrived(hbuf.at[0], s_spec.at[0])

    @pl.when(has_r)
    def _():
        arrived(hbuf.at[2], s_spec.at[1])

    for r, q in ((0, A_FWD), (128, A_TURN)):
        glift[r : r + 128, 0:256] += mm(hbuf[0], ta[q : q + 256, 256:512])
        glift[r : r + 128, 256:512] += mm(hbuf[2], ta[q : q + 256, 0:256])
    gl = glift[...].astype(BF16)

    gblk = [glift[:, 128 * i : 128 * i + 128] for i in range(4)]
    out_l = jnp.where(has_l, gblk[0], gblk[1]).astype(BF16)
    out_r = jnp.where(has_r, gblk[3], gblk[2]).astype(BF16)
    strip = mm(tb[pl.ds(pl.multiple_of(B_STRIP + EXT * c, 16), EXT)], jnp.concatenate([out_l, out_r], 1))
    pick_l = one_hot((16, 128), [(0, 0), (1, 1), (2, 0), (3, 1)])
    pick_r = one_hot((16, 128), [(0, 126), (1, 127), (2, 126), (3, 127)])
    picked = jnp.concatenate([mm_nt(pick_l, gl[:, 128:256]), mm_nt(pick_r, gl[:, 256:384])], 0)
    crossed = mm(picked.astype(BF16), tb[pl.ds(pl.multiple_of(B_CROSS + 256 * c, 16), 256)])
    row16 = lax.broadcasted_iota(jnp.int32, (16, 128), 0)
    ml = remote(19, msg_s.at[0], msg_r.at[1 - zl], s_msg.at[1 - zl], (ar, bl, c))
    mr = remote(20, msg_s.at[1], msg_r.at[zr], s_msg.at[zr], (ar, br, c))
    nl = remote(21, small_s.at[0], small_r.at[1 - zl], s_small.at[1 - zl], (ar, bl, other))
    nr = remote(22, small_s.at[1], small_r.at[zr], s_small.at[zr], (ar, br, other))

    @pl.when(hops)
    def _():
        pl.semaphore_wait(ready, 4)

    for side in range(2):
        cols = slice(128 * side, 128 * side + 128)
        cr = crossed[16 * side : 16 * side + 16]
        edge = jnp.where(row16 < 2, cr[:, :128], cr[:, 128:])[0:8]
        part = strip[:, cols]
        near_rows = jnp.where(is0, part[8:16], part[0:8])
        msg_s[side, 0:16] = jnp.concatenate([edge, near_rows], 0).astype(BF16)
        msg_s[side, 16:EXT] = part[16:EXT].astype(BF16)
        tail_rows = jnp.where(is0, part[136:144], part[16:24])
        small_s[side] = jnp.concatenate([edge, tail_rows], 0).astype(BF16)
        start(send_ok, *((ml, nl), (mr, nr))[side])


    ring_lane = lax.broadcasted_iota(jnp.int32, (256, 128), 1)
    gl_ring = jnp.where(ring_lane < 64, gblk[3], gblk[0]).astype(BF16)
    own_rows = tb[pl.ds(pl.multiple_of(B_OWN + EXT * c, 16), EXT)]
    grad = mm(own_rows, jnp.concatenate([gl[:, 128:384], gl_ring], 1))

    @pl.when(recv_ok)
    def _():
        arrived(msg_r.at[0], s_msg.at[0])
        arrived(msg_r.at[1], s_msg.at[1])

    @pl.when(small_ok)
    def _():
        arrived(small_r.at[0], s_small.at[0])
        arrived(small_r.at[1], s_small.at[1])

    eye = one_hot((128, 128), [])
    r128 = lax.broadcasted_iota(jnp.int32, (128, 128), 0)
    c128 = lax.broadcasted_iota(jnp.int32, (128, 128), 1)
    eye = jnp.where(r128 == c128, 1.0, 0.0).astype(BF16)
    sel_a = one_hot((32, 128), [(0, 126), (1, 127), (16, 0), (17, 1)])
    sel_b = one_hot((32, 128), [(2, 126), (3, 127), (18, 0), (19, 1)])
    edges = jnp.concatenate([msg_r[0, 0:16], msg_r[1, 0:16]], 0)
    edges_s = jnp.concatenate([small_r[0], small_r[1]], 0)
    turned = mm_nt(eye, edges).astype(BF16)
    turned_s = mm_nt(eye, edges_s).astype(BF16)
    col_main = mm(turned, sel_a)
    col_far = mm(turned, sel_b)
    col_small = mm(turned_s, sel_a)

    def add_part(blocks_main, blocks_ext, blocks_small):
        main = jnp.concatenate(blocks_main, 1)
        far = jnp.concatenate(blocks_ext, 1)
        near = jnp.concatenate(blocks_small, 1)
        after = jnp.where(is0, near[0:8], far[0:8])
        before = jnp.where(is0, far[8:16], near[8:16])
        return jnp.concatenate([main, after, before], 0)

    def twice(x):
        rows = x.astype(F32)[8:16]
        return jnp.concatenate([rows, rows], 0)

    col_far16 = jnp.concatenate([col_far[0:8], col_far[120:128]], 0)
    col_small16 = jnp.concatenate([col_small[0:8], col_small[120:128]], 0)
    received = add_part(
        [msg_r[0, 16:EXT].astype(F32), msg_r[1, 16:EXT].astype(F32), col_main],
        [twice(msg_r[0, 0:16]), twice(msg_r[1, 0:16]), col_far16],
        [twice(small_r[0]), twice(small_r[1]), col_small16],
    )
    speed = SPEED_GAIN * (grad + received) * final[:, LANES : 2 * LANES]

    row = lax.broadcasted_iota(jnp.int32, (EXT, LANES), 0)
    col = lax.broadcasted_iota(jnp.int32, (EXT, LANES), 1)
    i_off = jnp.where(row < 136, row, row - EXT) + 128 * c
    j_off = jnp.where(col < 320, col, col - LANES)
    i_all = a * TILE + i_off
    j_all = b * TILE + j_off
    inside = (i_all >= 0) & (i_all < n_ty * TILE) & (j_all >= 0) & (j_all < n_tx * TILE)

    level = final[:, 0:LANES]
    for _ in range(LS_STEPS):
        up = pltpu.roll(level, 1, 0)
        down = pltpu.roll(level, EXT - 1, 0)
        lf = pltpu.roll(level, 1, 1)
        rt = pltpu.roll(level, LANES - 1, 1)
        sy = 0.5 * (down - up)
        sx = 0.5 * (rt - lf)
        spread = up + down + lf + rt - 4.0 * level
        level = level - speed * jnp.sqrt(GRAD_FLOOR + sy * sy + sx * sx) + SMOOTHING * spread
        level = jnp.where(inside, level, 0.0)
    final[0:128, 0:256] = level[0:128, 0:256]

    mine = out_hbm.at[pl.ds(pl.multiple_of(128 * c, 128), 128)]
    result = final.at[pl.ds(0, 128), pl.ds(0, 256)]
    ff = remote(23, result, mine, s_final, partner)
    ff.start()
    started.append((c >= 0, (ff,)))
    cp_out = local(result, mine, out_sem.at[1])

    cp_resist.wait()
    cp_out.wait()
    settle()
    arrived(out_hbm.at[pl.ds(pl.multiple_of(128 * other, 128), 128)], s_final)


def make_body(n_ty, n_tx):
    def body(level_init, target, kernels, corner_doses):
        ta, tb = wide_tables()
        dma = pltpu.SemaphoreType.DMA
        anywhere = pl.BlockSpec(memory_space=pl.ANY)

        def whole(*args):
            return kernel(n_ty, n_tx, *args)

        return pl.pallas_call(
            whole,
            out_shape=(
                jax.ShapeDtypeStruct((1, TILE, TILE), F32),
                jax.ShapeDtypeStruct((TILE, TILE), F32),
            ),
            in_specs=[
                anywhere,
                anywhere,
                anywhere,
                pl.BlockSpec(memory_space=pltpu.SMEM),
                anywhere,
                anywhere,
            ],
            out_specs=(anywhere, anywhere),
            scratch_shapes=[
                pltpu.VMEM((TILE, TILE), jnp.int32),
                pltpu.VMEM((TILE, TILE), jnp.int32),
                pltpu.VMEM((1, KERNELS, 2, KF, KF), F32),
                pltpu.VMEM((A_ROWS, 512), BF16),
                pltpu.VMEM((B_ROWS, 256), BF16),
                pltpu.VMEM((4, WIN, 128), BF16),
                pltpu.VMEM((WIN, WIN), BF16),
                pltpu.VMEM((2, KF, KF), F32),
                pltpu.VMEM((KERNELS, TILE, 2 * TILE), F32),
                pltpu.VMEM((KERNELS * TILE, TILE), BF16),
                pltpu.VMEM((TILE, TILE), F32),
                pltpu.VMEM((TILE, TILE), F32),
                pltpu.VMEM((TILE, TILE), F32),
                pltpu.VMEM((KF, 2 * KF), F32),
                pltpu.VMEM((KF, 2 * KF), F32),
                pltpu.VMEM((3, KF, 2 * KF), BF16),
                pltpu.VMEM((2 * KF, WIN), F32),
                pltpu.VMEM((2 * KF, WIN), F32),
                pltpu.VMEM((2, EXT, 128), BF16),
                pltpu.VMEM((2, EXT, 128), BF16),
                pltpu.VMEM((2, 16, 128), BF16),
                pltpu.VMEM((2, 16, 128), BF16),
                pltpu.VMEM((EXT, 2 * LANES), F32),
                pltpu.VMEM((2, 128, 128), BF16),
                dma((5,)),
                dma((2,)),
                dma((28,)),
                dma((2,)),
                dma((2,)),
                dma((2, 2)),
                dma((2,)),
                dma,
                dma((2,)),
                dma((2,)),
                dma((2,)),
                dma,
                dma((2,)),
                pltpu.SemaphoreType.REGULAR,
                pltpu.SemaphoreType.REGULAR,
            ],
            compiler_params=pltpu.CompilerParams(
                collective_id=0,
                has_side_effects=True,
                vmem_limit_bytes=54600 * 1024,
            ),
            cost_estimate=pl.CostEstimate(
                flops=1_500_000_000, bytes_accessed=6_000_000, transcendentals=400_000
            ),
        )(level_init, target, kernels, corner_doses, jnp.asarray(ta), jnp.asarray(tb))

    return body


def solution(mesh):
    in_specs = (P("ty", "tx"), P("ty", "tx"), P("corner", None, None, None, None), P("corner"))
    out_specs = (P("corner", "ty", "tx"), P("ty", "tx"))
    return jax.shard_map(
        make_body(mesh.shape["ty"], mesh.shape["tx"]),
        mesh=mesh,
        in_specs=in_specs,
        out_specs=out_specs,
        check_vma=False,
    )
```
